32 devices in a mesh: section: 4 (over x, core), vocab: 8 (over z, y).
Axes of the slice: x: 2, y: 2, z: 4, core: 2. Of those that a mesh axis runs over, the one named last changes fastest.
Arguments:
- token_grad: bfloat16 [8192, 4608], P('vocab', 'section'), may hold values from -6 to 6
- token_ids: int32 [8192], P('vocab'), may hold values from -1 to 519, as said below
- block_counts: int32 [8, 8], P('vocab'), may hold values from 0 to 2, as said below
- hidden: bfloat16 [2048, 4608], P('section'), may hold values from -6 to 6
- dlogits: bfloat16 [2048, 4160], P('section', 'vocab'), may hold values from -0.125 to 0.125
- master: float32 [4160, 4608], P('vocab', 'section'), may hold values from -0.046875 to 0.046875
- moment1: float32 [4160, 4608], P('vocab', 'section'), may hold values from -4 to 4
- moment2: float32 [4160, 4608], P('vocab', 'section'), may hold values from 0.01 to 1
Outputs:
- new_master: float32 [4160, 4608], P('vocab', 'section')
- new_moment1: float32 [4160, 4608], P('vocab', 'section')
- new_moment2: float32 [4160, 4608], P('vocab', 'section')
- refreshed: bfloat16 [4160, 4608], P('vocab')
The draws below stay inside these ranges and needn't reach their ends.
Inputs may be any that keep to these rules, and one draw needn't show every extreme that they name: `block_counts`: row j gives, for each owner in order, how many of sender j's 8 blocks belong to it; each row sums to 8 and sender j's blocks come in owner order; one owner gets 2 blocks from every sender. `token_ids`: an id is a row among its block's owner's 520 rows, or -1 for a padding row.
All inputs are finite; a program needn't handle non-finite values.
Results may differ from the reference program's by a relative error of at most 0.005.
Values may be sent and summed in bfloat16 or wider, within the bound.
A program may use at most 128 MiB of HBM per device.

```python
import math
import jax
import jax.numpy as jnp
from jax import lax

D = 4608
VROWS_DEV = 520
BLOCK = 128
BLK_DEV = 8
OWNERS = 8
CAP = 2
V = 4160
TOKENS = 8192
HTOK = 2048


def draw_block_counts(key, part):
    key = jax.random.fold_in(key, 5)
    heat_key, noise_key, favor_key = jax.random.split(key, 3)
    slot_total = OWNERS * CAP
    slot_owner = jnp.arange(slot_total, dtype=jnp.int32) // CAP
    heat_level = jax.random.randint(heat_key, (OWNERS,), 0, 4, dtype=jnp.int32)
    favored = jax.random.randint(favor_key, (), 0, OWNERS, dtype=jnp.int32)
    noise_score = jax.random.randint(noise_key, (OWNERS, slot_total), 0, 4096, dtype=jnp.int32)
    weight = heat_level[slot_owner] * 1024 + 16384 * (slot_owner == favored).astype(jnp.int32)
    slot_score = (weight[None, :] + noise_score) * slot_total + jnp.arange(slot_total, dtype=jnp.int32)[None, :]
    _, chosen = lax.top_k(slot_score, BLK_DEV)
    chosen_owner = slot_owner[chosen]
    owner_list = jnp.arange(OWNERS, dtype=jnp.int32)
    counts = jnp.sum((chosen_owner[:, :, None] == owner_list[None, None, :]).astype(jnp.int32), axis=1)
    return counts.astype(jnp.int32)


def draw_token_ids(key, part):
    key = jax.random.fold_in(key, 9)
    raw_key, offset_key, padded_key = jax.random.split(key, 3)
    raw_index = jax.random.randint(raw_key, (TOKENS,), 0, VROWS_DEV, dtype=jnp.int32)
    skewed = raw_index * raw_index // VROWS_DEV
    offset = jax.random.randint(offset_key, (TOKENS // BLOCK, 1), 0, VROWS_DEV, dtype=jnp.int32)
    local_id = ((skewed.reshape(-1, BLOCK) + offset) % VROWS_DEV).reshape(-1)
    padded = jax.random.randint(padded_key, (TOKENS,), 0, 4, dtype=jnp.int32) == 0
    return jnp.where(padded, -1, local_id).astype(jnp.int32)


def levels(rng, extent, shards, smallest, high):
    factor_of = 1.0
    for axis_at, shards_of in shards:
        draws = jax.random.uniform(jax.random.fold_in(jax.random.fold_in(rng, 6), axis_at), (shards_of,), jnp.float32, smallest / len(shards), high / len(shards))
        factor_of = factor_of * jnp.repeat(jnp.exp(draws), extent[axis_at] // shards_of).reshape((-1,) + (1,) * (len(extent) - 1 - axis_at))
    return factor_of


def noise(stream_key, shape, scale, limit, shards=(), held_as=jnp.bfloat16):
    values = jax.random.normal(stream_key, shape, jnp.float32) * scale
    if len(shards) > 0:
        values = levels(stream_key, shape, shards, -0.22, 0.18) * values
    return jnp.clip(values, min=-limit, max=limit).astype(held_as)


def setup_inputs(seed: int = 0) -> dict:
    splits = jax.random.split(jax.random.key(seed), 9)
    token_grad = noise(splits[0], (TOKENS, D), 1.0, 6.0, ((0, 8), (1, 4)))
    token_ids = draw_token_ids(jax.random.fold_in(splits[8], 71), 0)
    block_counts = draw_block_counts(jax.random.fold_in(splits[8], 71), 0)
    hidden = noise(splits[3], (HTOK, D), 1.0, 6.0, ((0, 4),))
    dlogits = noise(splits[4], (HTOK, V), HTOK ** -0.5, 0.125, ((0, 4), (1, 8)))
    master = noise(splits[5], (V, D), 0.003, 0.046875, ((0, 8), (1, 4)), jnp.float32)
    moment1 = noise(splits[6], (V, D), 0.3, 4.0, ((0, 8), (1, 4)), jnp.float32)
    moment2 = jnp.clip(jnp.exp(math.log(1.0) - 4.6051702 * jax.random.uniform(splits[7], (V, D), jnp.float32) ** levels(splits[7], (V, D), ((0, 8), (1, 4)), -0.2, 0.2)), 0.01, 1.0)
    return {"token_grad": token_grad, "token_ids": token_ids, "block_counts": block_counts, "hidden": hidden, "dlogits": dlogits, "master": master, "moment1": moment1, "moment2": moment2}


beta_first = 0.9
beta_second = 0.999
learn_rate = 0.01
adam_epsilon = 1e-08
first_fix = 1.0 - 0.9 ** 10
second_fix = 1.0 - 0.999 ** 10

def reference(token_grad, token_ids, block_counts, hidden, dlogits, master, moment1, moment2):
    count_ends = jnp.cumsum(block_counts, axis=1).astype(jnp.int32)
    block_index = jnp.arange(BLK_DEV, dtype=jnp.int32)
    owner_of_block = lax.optimization_barrier(jnp.sum((count_ends[:, None, :] <= block_index[None, :, None]).astype(jnp.int32), axis=2))
    row_owner = jnp.repeat(owner_of_block.reshape(-1), BLOCK).astype(jnp.int32)
    slab_id = jnp.where(token_ids >= 0, row_owner * VROWS_DEV + token_ids, V).astype(jnp.int32)
    token_sum = jax.ops.segment_sum(token_grad.astype(jnp.float32), slab_id, num_segments=V + 1)[:V]
    head_grad = jnp.dot(dlogits.T, hidden, preferred_element_type=jnp.float32)
    gradient = token_sum + head_grad
    new_moment1 = beta_first * moment1 + (1.0 - beta_first) * gradient
    new_moment2 = beta_second * moment2 + (1.0 - beta_second) * gradient * gradient
    new_master = master - learn_rate * (new_moment1 / first_fix) / (jnp.sqrt(new_moment2 / second_fix) + adam_epsilon)
    return (new_master, new_moment1, new_moment2, new_master.astype(jnp.bfloat16))
```

```python
import jax
import jax.numpy as jnp
from jax import lax
from jax.sharding import PartitionSpec as P

BLOCK = 128
CHUNKS = 3


beta_first = 0.9
beta_second = 0.999
learn_rate = 0.01
adam_epsilon = 1e-08
first_fix = 1.0 - 0.9**10
second_fix = 1.0 - 0.999**10


def shards(token_grad, token_ids, block_counts, hidden, dlogits, master, moment1, moment2):
    owners = lax.axis_size("vocab")
    sections = lax.axis_size("section")
    me = lax.axis_index("vocab")
    row_total, quarter = token_grad.shape
    block_total = row_total // BLOCK
    capacity = max(1, 2 * block_total // owners)
    slab_rows = master.shape[0]
    chunk = quarter // CHUNKS
    counts = block_counts[0]
    starts = jnp.cumsum(counts) - counts
    slot_index = jnp.arange(capacity, dtype=jnp.int32)
    live_slot = slot_index[None, :] < counts[:, None]
    pick_index = jnp.where(live_slot, starts[:, None] + slot_index[None, :], 0)
    grad_blocks = token_grad.reshape(block_total, BLOCK, quarter)
    picked = pick_index.reshape(-1)
    got_rows = []
    for c in range(CHUNKS):
        send = grad_blocks[:, :, c * chunk : (c + 1) * chunk][picked].reshape(
            owners, capacity * BLOCK, chunk
        )
        got_rows.append(
            lax.all_to_all(send, "vocab", split_axis=0, concat_axis=0, tiled=True).reshape(-1, chunk)
        )
    id_blocks = token_ids.reshape(block_total, BLOCK)
    packed = jnp.concatenate([id_blocks, jnp.pad(counts, (0, BLOCK - owners))[None]], axis=0)
    everyone = lax.all_gather(packed, "vocab", axis=0, tiled=False)
    all_counts = everyone[:, block_total, :owners]
    before = jnp.arange(owners) < me
    my_start = jnp.sum(jnp.where(before[None, :], all_counts, 0), axis=1)
    my_count = jnp.sum(jnp.where((jnp.arange(owners) == me)[None, :], all_counts, 0), axis=1)
    fills = (
        (my_start[:, None] + slot_index[None, :])[:, :, None]
        == jnp.arange(block_total)[None, None, :]
    ) & (slot_index[None, :] < my_count[:, None])[:, :, None]
    flat_ids = (
        jnp.sum(
            jnp.where(fills[:, :, :, None], everyone[:, None, :block_total] + 1, 0), axis=2
        )
        - 1
    ).reshape(-1)
    one_hot = (jnp.arange(slab_rows, dtype=jnp.int32)[:, None] == flat_ids[None, :]).astype(
        jnp.bfloat16
    )
    parts = jnp.stack(
        [
            lax.dot_general(
                dlogits,
                hidden[:, q * quarter : (q + 1) * quarter],
                (((0,), (0,)), ((), ())),
                preferred_element_type=jnp.float32,
            ).astype(jnp.bfloat16)
            for q in range(sections)
        ]
    )
    head = lax.psum_scatter(parts, "section", scatter_dimension=0, tiled=False)
    outs = []
    for c in range(CHUNKS):
        cols = slice(c * chunk, (c + 1) * chunk)
        token_sum = jnp.dot(one_hot, got_rows[c], preferred_element_type=jnp.float32)
        gradient = token_sum + head[:, cols].astype(jnp.float32)
        new_moment1 = beta_first * moment1[:, cols] + (1.0 - beta_first) * gradient
        new_moment2 = beta_second * moment2[:, cols] + (1.0 - beta_second) * gradient * gradient
        new_master = master[:, cols] - learn_rate * (new_moment1 / first_fix) / (
            jnp.sqrt(new_moment2 / second_fix) + adam_epsilon
        )
        shared = lax.all_gather(new_master.astype(jnp.bfloat16), "section", axis=0, tiled=False)
        outs.append((new_master, new_moment1, new_moment2, shared))
    refreshed = jnp.concatenate(
        [outs[c][3][q] for q in range(sections) for c in range(CHUNKS)], axis=1
    )
    return tuple(jnp.concatenate([o[i] for o in outs], axis=1) for i in range(3)) + (refreshed,)


def solution(mesh):
    placed = (
        P("vocab", "section"),
        P("vocab"),
        P("vocab", None),
        P("section", None),
        P("section", "vocab"),
        P("vocab", "section"),
        P("vocab", "section"),
        P("vocab", "section"),
    )
    return jax.shard_map(
        shards,
        mesh=mesh,
        in_specs=placed,
        out_specs=(
            P("vocab", "section"),
            P("vocab", "section"),
            P("vocab", "section"),
            P("vocab", None),
        ),
        check_vma=False,
    )
```

```python
import functools

import jax
import jax.numpy as jnp
from jax import lax
from jax.experimental import pallas as pl
from jax.experimental.pallas import tpu as pltpu
from jax.sharding import PartitionSpec as P

BLOCK = 128
LANES = 128
MESH = pl.DeviceIdType.MESH


beta_first = 0.9
beta_second = 0.999
learn_rate = 0.01
adam_epsilon = 1e-08
first_fix = 1.0 - 0.9**10
second_fix = 1.0 - 0.999**10


def kernel(
    owners, sections, capacity,
    counts_ref, ids_ref, grad_hbm, hidden_hbm, dlogits_hbm, master_hbm, moment1_hbm, moment2_hbm,
    master_out, moment1_out, moment2_out, refreshed_out,
    starts, grad, hidden, dlogits, master, moment1, moment2,
    id_send, id_got, row_send, row_got, one_hot, part, part_got, own_part, fresh, fresh_got,
    load_sem, store_sem, id_send_sem, id_recv_sem, row_send_sem, row_recv_sem,
    part_send_sem, part_recv_sem, fresh_send_sem, fresh_recv_sem,
):
    me = lax.axis_index("vocab")
    here = lax.axis_index("section")
    quarter = master.shape[1]
    chunks = quarter // LANES
    slab_rows = master.shape[0]

    loads = [
        pltpu.make_async_copy(source, target, load_sem.at[i])
        for i, (source, target) in enumerate(
            [
                (grad_hbm, grad),
                (dlogits_hbm, dlogits),
                (hidden_hbm, hidden),
                (master_hbm, master),
                (moment1_hbm, moment1),
                (moment2_hbm, moment2),
            ]
        )
    ]
    for load in loads:
        load.start()

    barrier = pltpu.get_barrier_semaphore()

    @pl.loop(1, owners)
    def _(d):
        pl.semaphore_signal(
            barrier, inc=1, device_id={"vocab": lax.rem(me + d, owners)}, device_id_type=MESH
        )

    @pl.loop(1, sections)
    def _(e):
        pl.semaphore_signal(
            barrier, inc=1, device_id={"section": lax.rem(here + e, sections)}, device_id_type=MESH
        )

    def add_start(o, total):
        starts[o] = total
        return total + counts_ref[0, o]

    lax.fori_loop(0, owners, add_start, jnp.int32(0))

    def pick(owner, slot):
        live = slot < counts_ref[0, owner]
        return live, jnp.where(live, starts[owner] + slot, 0)

    def fill_ids(owner, target):
        target[...] = jnp.full((8, BLOCK), -1, jnp.int32)
        for slot in range(capacity):
            live, block = pick(owner, slot)
            target[slot : slot + 1, :] = jnp.where(live, ids_ref[pl.ds(block, 1), :], -1)

    pl.semaphore_wait(barrier, owners - 1 + sections - 1)

    def id_copy(d):
        return pltpu.make_async_remote_copy(
            src_ref=id_send.at[d - 1],
            dst_ref=id_got.at[d - 1],
            send_sem=id_send_sem,
            recv_sem=id_recv_sem,
            device_id={"vocab": lax.rem(me + d, owners)},
            device_id_type=MESH,
        )

    @pl.loop(1, owners)
    def _(d):
        fill_ids(lax.rem(me + d, owners), id_send.at[d - 1])
        id_copy(d).start()

    fill_ids(me, id_got.at[owners - 1])

    loads[0].wait()

    def fill_rows(owner, c, target):
        for slot in range(capacity):
            _, block = pick(owner, slot)
            target[slot * BLOCK : (slot + 1) * BLOCK, :] = grad[
                block, :, pl.ds(pl.multiple_of(c * LANES, LANES), LANES)
            ]

    @pl.loop(0, chunks)
    def _(c):
        @pl.loop(1, owners)
        def _(d):
            owner = lax.rem(me + d, owners)
            fill_rows(owner, c, row_send.at[c, d - 1])
            pltpu.make_async_remote_copy(
                src_ref=row_send.at[c, d - 1],
                dst_ref=row_got.at[c, d - 1],
                send_sem=row_send_sem.at[c],
                recv_sem=row_recv_sem.at[c],
                device_id={"vocab": owner},
                device_id_type=MESH,
            ).start()

        fill_rows(me, c, row_got.at[c, owners - 1])

    loads[1].wait()
    loads[2].wait()

    def head_part(section, c):
        at = pl.multiple_of(section * quarter + c * LANES, LANES)
        return jnp.dot(
            dlogits[...], hidden[:, pl.ds(at, LANES)], preferred_element_type=jnp.float32
        )

    @pl.loop(0, chunks)
    def _(c):
        @pl.loop(1, sections)
        def _(e):
            section = lax.rem(here + e, sections)
            part[c, e - 1] = head_part(section, c).astype(jnp.bfloat16)
            pltpu.make_async_remote_copy(
                src_ref=part.at[c, e - 1],
                dst_ref=part_got.at[c, e - 1],
                send_sem=part_send_sem.at[c],
                recv_sem=part_recv_sem.at[c],
                device_id={"section": section},
                device_id_type=MESH,
            ).start()

        own_part[c] = head_part(here, c)

    arrived = id_got.at[pl.ds(0, owners - 1)]
    pltpu.make_async_copy(arrived, arrived, id_recv_sem).wait()

    @pl.loop(0, owners)
    def _(s):
        for slot in range(capacity):
            ids = id_got[s, slot : slot + 1, :]
            rows = lax.broadcasted_iota(jnp.int32, (slab_rows, BLOCK), 0)
            at = pl.multiple_of((s * capacity + slot) * BLOCK, BLOCK)
            one_hot[:, pl.ds(at, BLOCK)] = jnp.where(rows == ids, 1.0, 0.0).astype(jnp.bfloat16)

    for load in loads[3:]:
        load.wait()

    @pl.loop(0, chunks)
    def _(c):
        cols = pl.ds(pl.multiple_of(c * LANES, LANES), LANES)
        rows_in = row_got.at[c, pl.ds(0, owners - 1)]
        pltpu.make_async_copy(rows_in, rows_in, row_recv_sem.at[c]).wait()
        parts_in = part_got.at[c]
        pltpu.make_async_copy(parts_in, parts_in, part_recv_sem.at[c]).wait()
        gradient = jnp.dot(
            one_hot[...],
            row_got[c].reshape(owners * capacity * BLOCK, LANES),
            preferred_element_type=jnp.float32,
        )
        head = own_part[c]
        for e in range(sections - 1):
            head = head + part_got[c, e].astype(jnp.float32)
        gradient = gradient + head
        new_moment1 = beta_first * moment1[:, cols] + (1.0 - beta_first) * gradient
        new_moment2 = beta_second * moment2[:, cols] + (1.0 - beta_second) * gradient * gradient
        new_master = master[:, cols] - learn_rate * (new_moment1 / first_fix) / (
            jnp.sqrt(new_moment2 / second_fix) + adam_epsilon
        )
        fresh[c] = new_master.astype(jnp.bfloat16)

        @pl.loop(1, sections)
        def _(e):
            pltpu.make_async_remote_copy(
                src_ref=fresh.at[c],
                dst_ref=fresh_got.at[c, e - 1],
                send_sem=fresh_send_sem.at[c],
                recv_sem=fresh_recv_sem.at[c],
                device_id={"section": lax.rem(here + e, sections)},
                device_id_type=MESH,
            ).start()

        moment1[:, cols] = new_moment1
        moment2[:, cols] = new_moment2
        master[:, cols] = new_master
        pltpu.make_async_copy(master.at[:, cols], master_out.at[:, cols], store_sem.at[0]).start()
        pltpu.make_async_copy(moment1.at[:, cols], moment1_out.at[:, cols], store_sem.at[1]).start()
        pltpu.make_async_copy(moment2.at[:, cols], moment2_out.at[:, cols], store_sem.at[2]).start()
        at = pl.multiple_of(here * quarter + c * LANES, LANES)
        pltpu.make_async_copy(
            fresh.at[c], refreshed_out.at[:, pl.ds(at, LANES)], store_sem.at[3]
        ).start()

    @pl.loop(0, chunks)
    def _(c):
        fresh_in = fresh_got.at[c]
        pltpu.make_async_copy(fresh_in, fresh_in, fresh_recv_sem.at[c]).wait()

        @pl.loop(1, sections)
        def _(e):
            source = lax.rem(here + sections - e, sections)
            at = pl.multiple_of(source * quarter + c * LANES, LANES)
            pltpu.make_async_copy(
                fresh_got.at[c, e - 1], refreshed_out.at[:, pl.ds(at, LANES)], store_sem.at[3]
            ).start()

    pltpu.make_async_copy(id_send, id_send, id_send_sem).wait()

    @pl.loop(0, chunks)
    def _(c):
        pltpu.make_async_copy(row_send.at[c], row_send.at[c], row_send_sem.at[c]).wait()
        pltpu.make_async_copy(part.at[c], part.at[c], part_send_sem.at[c]).wait()
        pltpu.make_async_copy(fresh_got.at[c], fresh_got.at[c], fresh_send_sem.at[c]).wait()

    pltpu.make_async_copy(master, master_out, store_sem.at[0]).wait()
    pltpu.make_async_copy(moment1, moment1_out, store_sem.at[1]).wait()
    pltpu.make_async_copy(moment2, moment2_out, store_sem.at[2]).wait()
    pltpu.make_async_copy(refreshed_out, refreshed_out, store_sem.at[3]).wait()


def shards(token_grad, token_ids, block_counts, hidden, dlogits, master, moment1, moment2):
    owners = lax.axis_size("vocab")
    sections = lax.axis_size("section")
    row_total, quarter = token_grad.shape
    block_total = row_total // BLOCK
    capacity = max(1, 2 * block_total // owners)
    slab_rows = master.shape[0]
    tokens, width = hidden.shape
    chunks = quarter // LANES
    slots = capacity * BLOCK
    f32, bf16 = jnp.float32, jnp.bfloat16
    hbm = pl.BlockSpec(memory_space=pl.ANY)
    dma = pltpu.SemaphoreType.DMA
    slab = (slab_rows, quarter)
    return pl.pallas_call(
        functools.partial(kernel, owners, sections, capacity),
        out_shape=(
            jax.ShapeDtypeStruct(slab, f32),
            jax.ShapeDtypeStruct(slab, f32),
            jax.ShapeDtypeStruct(slab, f32),
            jax.ShapeDtypeStruct((slab_rows, width), bf16),
        ),
        in_specs=[
            pl.BlockSpec(memory_space=pltpu.SMEM),
            pl.BlockSpec(memory_space=pltpu.VMEM),
            hbm, hbm, hbm, hbm, hbm, hbm,
        ],
        out_specs=(hbm, hbm, hbm, hbm),
        scratch_shapes=[
            pltpu.SMEM((owners,), jnp.int32),
            pltpu.VMEM((block_total, BLOCK, quarter), bf16),
            pltpu.VMEM((tokens, width), bf16),
            pltpu.VMEM((slab_rows, tokens), bf16),
            pltpu.VMEM(slab, f32),
            pltpu.VMEM(slab, f32),
            pltpu.VMEM(slab, f32),
            pltpu.VMEM((owners - 1, 8, BLOCK), jnp.int32),
            pltpu.VMEM((owners, 8, BLOCK), jnp.int32),
            pltpu.VMEM((chunks, owners - 1, slots, LANES), bf16),
            pltpu.VMEM((chunks, owners, slots, LANES), bf16),
            pltpu.VMEM((slab_rows, owners * slots), bf16),
            pltpu.VMEM((chunks, sections - 1, slab_rows, LANES), bf16),
            pltpu.VMEM((chunks, sections - 1, slab_rows, LANES), bf16),
            pltpu.VMEM((chunks, slab_rows, LANES), f32),
            pltpu.VMEM((chunks, slab_rows, LANES), bf16),
            pltpu.VMEM((chunks, sections - 1, slab_rows, LANES), bf16),
            dma((6,)),
            dma((4,)),
            dma,
            dma,
            dma((chunks,)),
            dma((chunks,)),
            dma((chunks,)),
            dma((chunks,)),
            dma((chunks,)),
            dma((chunks,)),
        ],
        compiler_params=pltpu.CompilerParams(
            collective_id=0, has_side_effects=True, vmem_limit_bytes=58 * 1024 * 1024
        ),
    )(
        block_counts,
        token_ids.reshape(block_total, BLOCK),
        token_grad.reshape(block_total, BLOCK, quarter),
        hidden,
        dlogits.T,
        master,
        moment1,
        moment2,
    )


def solution(mesh):
    placed = (
        P("vocab", "section"),
        P("vocab"),
        P("vocab", None),
        P("section", None),
        P("section", "vocab"),
        P("vocab", "section"),
        P("vocab", "section"),
        P("vocab", "section"),
    )
    return jax.shard_map(
        shards,
        mesh=mesh,
        in_specs=placed,
        out_specs=(
            P("vocab", "section"),
            P("vocab", "section"),
            P("vocab", "section"),
            P("vocab", None),
        ),
        check_vma=False,
    )
```

```python
import functools

import jax
import jax.numpy as jnp
from jax import lax
from jax.experimental import pallas as pl
from jax.experimental.pallas import tpu as pltpu
from jax.sharding import PartitionSpec as P

BLOCK = 128
LANES = 128
MESH = pl.DeviceIdType.MESH


beta_first = 0.9
beta_second = 0.999
learn_rate = 0.01
adam_epsilon = 1e-08
first_fix = 1.0 - 0.9**10
second_fix = 1.0 - 0.999**10


def direct_kernel(
    owners, sections, capacity,
    counts_ref, ids_ref, grad_hbm, hidden_hbm, dlogits_hbm, master_hbm, moment1_hbm, moment2_hbm,
    master_out, moment1_out, moment2_out, refreshed_out,
    starts, grad, hidden, dlogits, master, moment1, moment2,
    id_send, id_got, row_send, row_got, one_hot, part, part_got, own_part, fresh, fresh_got,
    load_sem, store_sem, id_send_sem, id_recv_sem, row_send_sem, row_recv_sem,
    part_send_sem, part_recv_sem, fresh_send_sem, fresh_recv_sem,
):
    me = lax.axis_index("vocab")
    here = lax.axis_index("section")
    quarter = master.shape[1]
    chunks = quarter // LANES
    slab_rows = master.shape[0]

    loads = [
        pltpu.make_async_copy(source, target, load_sem.at[i])
        for i, (source, target) in enumerate(
            [
                (grad_hbm, grad),
                (dlogits_hbm, dlogits),
                (hidden_hbm, hidden),
                (master_hbm, master),
                (moment1_hbm, moment1),
                (moment2_hbm, moment2),
            ]
        )
    ]
    for load in loads:
        load.start()

    barrier = pltpu.get_barrier_semaphore()

    @pl.loop(1, owners)
    def _(d):
        pl.semaphore_signal(
            barrier, inc=1, device_id={"vocab": lax.rem(me + d, owners)}, device_id_type=MESH
        )

    @pl.loop(1, sections)
    def _(e):
        pl.semaphore_signal(
            barrier, inc=1, device_id={"section": lax.rem(here + e, sections)}, device_id_type=MESH
        )

    def add_start(o, total):
        starts[o] = total
        return total + counts_ref[0, o]

    lax.fori_loop(0, owners, add_start, jnp.int32(0))

    def pick(owner, slot):
        live = slot < counts_ref[0, owner]
        return live, jnp.where(live, starts[owner] + slot, 0)

    def fill_ids(owner, target):
        target[...] = jnp.full((8, BLOCK), -1, jnp.int32)
        for slot in range(capacity):
            live, block = pick(owner, slot)
            target[slot : slot + 1, :] = jnp.where(live, ids_ref[pl.ds(block, 1), :], -1)

    pl.semaphore_wait(barrier, owners - 1 + sections - 1)

    def id_copy(d):
        return pltpu.make_async_remote_copy(
            src_ref=id_send.at[d - 1],
            dst_ref=id_got.at[d - 1],
            send_sem=id_send_sem,
            recv_sem=id_recv_sem,
            device_id={"vocab": lax.rem(me + d, owners)},
            device_id_type=MESH,
        )

    @pl.loop(1, owners)
    def _(d):
        fill_ids(lax.rem(me + d, owners), id_send.at[d - 1])
        id_copy(d).start()

    fill_ids(me, id_got.at[owners - 1])

    loads[0].wait()

    def fill_rows(owner, c, target):
        for slot in range(capacity):
            _, block = pick(owner, slot)
            target[slot * BLOCK : (slot + 1) * BLOCK, :] = grad[
                block, :, pl.ds(pl.multiple_of(c * LANES, LANES), LANES)
            ]

    @pl.loop(0, chunks)
    def _(c):
        @pl.loop(1, owners)
        def _(d):
            owner = lax.rem(me + d, owners)
            fill_rows(owner, c, row_send.at[c, d - 1])
            pltpu.make_async_remote_copy(
                src_ref=row_send.at[c, d - 1],
                dst_ref=row_got.at[c, d - 1],
                send_sem=row_send_sem.at[c],
                recv_sem=row_recv_sem.at[c],
                device_id={"vocab": owner},
                device_id_type=MESH,
            ).start()

        fill_rows(me, c, row_got.at[c, owners - 1])

    loads[1].wait()
    loads[2].wait()

    def head_part(section, c):
        at = pl.multiple_of(section * quarter + c * LANES, LANES)
        return jnp.dot(
            dlogits[...], hidden[:, pl.ds(at, LANES)], preferred_element_type=jnp.float32
        )

    @pl.loop(0, chunks)
    def _(c):
        @pl.loop(1, sections)
        def _(e):
            section = lax.rem(here + e, sections)
            part[c, e - 1] = head_part(section, c).astype(jnp.bfloat16)
            pltpu.make_async_remote_copy(
                src_ref=part.at[c, e - 1],
                dst_ref=part_got.at[c, e - 1],
                send_sem=part_send_sem.at[c],
                recv_sem=part_recv_sem.at[c],
                device_id={"section": section},
                device_id_type=MESH,
            ).start()

        own_part[c] = head_part(here, c)

    arrived = id_got.at[pl.ds(0, owners - 1)]
    pltpu.make_async_copy(arrived, arrived, id_recv_sem).wait()

    @pl.loop(0, owners)
    def _(s):
        for slot in range(capacity):
            ids = id_got[s, slot : slot + 1, :]
            rows = lax.broadcasted_iota(jnp.int32, (slab_rows, BLOCK), 0)
            at = pl.multiple_of((s * capacity + slot) * BLOCK, BLOCK)
            one_hot[:, pl.ds(at, BLOCK)] = jnp.where(rows == ids, 1.0, 0.0).astype(jnp.bfloat16)

    for load in loads[3:]:
        load.wait()

    @pl.loop(0, chunks)
    def _(c):
        cols = pl.ds(pl.multiple_of(c * LANES, LANES), LANES)
        rows_in = row_got.at[c, pl.ds(0, owners - 1)]
        pltpu.make_async_copy(rows_in, rows_in, row_recv_sem.at[c]).wait()
        parts_in = part_got.at[c]
        pltpu.make_async_copy(parts_in, parts_in, part_recv_sem.at[c]).wait()
        gradient = jnp.dot(
            one_hot[...],
            row_got[c].reshape(owners * capacity * BLOCK, LANES),
            preferred_element_type=jnp.float32,
        )
        head = own_part[c]
        for e in range(sections - 1):
            head = head + part_got[c, e].astype(jnp.float32)
        gradient = gradient + head
        new_moment1 = beta_first * moment1[:, cols] + (1.0 - beta_first) * gradient
        new_moment2 = beta_second * moment2[:, cols] + (1.0 - beta_second) * gradient * gradient
        new_master = master[:, cols] - learn_rate * (new_moment1 / first_fix) / (
            jnp.sqrt(new_moment2 / second_fix) + adam_epsilon
        )
        fresh[c] = new_master.astype(jnp.bfloat16)

        @pl.loop(1, sections)
        def _(e):
            pltpu.make_async_remote_copy(
                src_ref=fresh.at[c],
                dst_ref=fresh_got.at[c, e - 1],
                send_sem=fresh_send_sem.at[c],
                recv_sem=fresh_recv_sem.at[c],
                device_id={"section": lax.rem(here + e, sections)},
                device_id_type=MESH,
            ).start()

        moment1[:, cols] = new_moment1
        moment2[:, cols] = new_moment2
        master[:, cols] = new_master
        pltpu.make_async_copy(master.at[:, cols], master_out.at[:, cols], store_sem.at[0]).start()
        pltpu.make_async_copy(moment1.at[:, cols], moment1_out.at[:, cols], store_sem.at[1]).start()
        pltpu.make_async_copy(moment2.at[:, cols], moment2_out.at[:, cols], store_sem.at[2]).start()
        at = pl.multiple_of(here * quarter + c * LANES, LANES)
        pltpu.make_async_copy(
            fresh.at[c], refreshed_out.at[:, pl.ds(at, LANES)], store_sem.at[3]
        ).start()

    @pl.loop(0, chunks)
    def _(c):
        fresh_in = fresh_got.at[c]
        pltpu.make_async_copy(fresh_in, fresh_in, fresh_recv_sem.at[c]).wait()

        @pl.loop(1, sections)
        def _(e):
            source = lax.rem(here + sections - e, sections)
            at = pl.multiple_of(source * quarter + c * LANES, LANES)
            pltpu.make_async_copy(
                fresh_got.at[c, e - 1], refreshed_out.at[:, pl.ds(at, LANES)], store_sem.at[3]
            ).start()

    pltpu.make_async_copy(id_send, id_send, id_send_sem).wait()

    @pl.loop(0, chunks)
    def _(c):
        pltpu.make_async_copy(row_send.at[c], row_send.at[c], row_send_sem.at[c]).wait()
        pltpu.make_async_copy(part.at[c], part.at[c], part_send_sem.at[c]).wait()
        pltpu.make_async_copy(fresh_got.at[c], fresh_got.at[c], fresh_send_sem.at[c]).wait()

    pltpu.make_async_copy(master, master_out, store_sem.at[0]).wait()
    pltpu.make_async_copy(moment1, moment1_out, store_sem.at[1]).wait()
    pltpu.make_async_copy(moment2, moment2_out, store_sem.at[2]).wait()
    pltpu.make_async_copy(refreshed_out, refreshed_out, store_sem.at[3]).wait()


def direct_shards(token_grad, token_ids, block_counts, hidden, dlogits, master, moment1, moment2):
    owners = lax.axis_size("vocab")
    sections = lax.axis_size("section")
    row_total, quarter = token_grad.shape
    block_total = row_total // BLOCK
    capacity = max(1, 2 * block_total // owners)
    slab_rows = master.shape[0]
    tokens, width = hidden.shape
    chunks = quarter // LANES
    slots = capacity * BLOCK
    f32, bf16 = jnp.float32, jnp.bfloat16
    hbm = pl.BlockSpec(memory_space=pl.ANY)
    dma = pltpu.SemaphoreType.DMA
    slab = (slab_rows, quarter)
    return pl.pallas_call(
        functools.partial(direct_kernel, owners, sections, capacity),
        out_shape=(
            jax.ShapeDtypeStruct(slab, f32),
            jax.ShapeDtypeStruct(slab, f32),
            jax.ShapeDtypeStruct(slab, f32),
            jax.ShapeDtypeStruct((slab_rows, width), bf16),
        ),
        in_specs=[
            pl.BlockSpec(memory_space=pltpu.SMEM),
            pl.BlockSpec(memory_space=pltpu.VMEM),
            hbm, hbm, hbm, hbm, hbm, hbm,
        ],
        out_specs=(hbm, hbm, hbm, hbm),
        scratch_shapes=[
            pltpu.SMEM((owners,), jnp.int32),
            pltpu.VMEM((block_total, BLOCK, quarter), bf16),
            pltpu.VMEM((tokens, width), bf16),
            pltpu.VMEM((slab_rows, tokens), bf16),
            pltpu.VMEM(slab, f32),
            pltpu.VMEM(slab, f32),
            pltpu.VMEM(slab, f32),
            pltpu.VMEM((owners - 1, 8, BLOCK), jnp.int32),
            pltpu.VMEM((owners, 8, BLOCK), jnp.int32),
            pltpu.VMEM((chunks, owners - 1, slots, LANES), bf16),
            pltpu.VMEM((chunks, owners, slots, LANES), bf16),
            pltpu.VMEM((slab_rows, owners * slots), bf16),
            pltpu.VMEM((chunks, sections - 1, slab_rows, LANES), bf16),
            pltpu.VMEM((chunks, sections - 1, slab_rows, LANES), bf16),
            pltpu.VMEM((chunks, slab_rows, LANES), f32),
            pltpu.VMEM((chunks, slab_rows, LANES), bf16),
            pltpu.VMEM((chunks, sections - 1, slab_rows, LANES), bf16),
            dma((6,)),
            dma((4,)),
            dma,
            dma,
            dma((chunks,)),
            dma((chunks,)),
            dma((chunks,)),
            dma((chunks,)),
            dma((chunks,)),
            dma((chunks,)),
        ],
        compiler_params=pltpu.CompilerParams(
            collective_id=0, has_side_effects=True, vmem_limit_bytes=58 * 1024 * 1024
        ),
    )(
        block_counts,
        token_ids.reshape(block_total, BLOCK),
        token_grad.reshape(block_total, BLOCK, quarter),
        hidden,
        dlogits.T,
        master,
        moment1,
        moment2,
    )


def relay_kernel(
    capacity,
    counts_ref, ids_ref, grad_hbm, hidden_hbm, dlogits_hbm, master_hbm, moment1_hbm, moment2_hbm,
    master_out, moment1_out, moment2_out, refreshed_out,
    starts, grad, hidden, dlogits, master, moment1, moment2,
    slab_ids, id_send, id_got, slot_send, slot_got, raw_got,
    own_hot, raw_hot, slot_hot, far_hot, total, far_keep, relay_send, relay_got, far_send, far_got,
    pair_send, pair_got, cross_send, cross_got, own_part, fresh, fresh_got,
    load_sem, store_sem, id_sems, slot_sems, raw_sems, relay_sems, far_sems,
    pair_sems, cross_sems, side_sems, over_sems, forward_sems,
):
    owners = counts_ref.shape[1]
    me = lax.axis_index("vocab")
    here = lax.axis_index("section")
    z, y = me // 2, lax.rem(me, 2)
    mate_z = z + 1 - 2 * lax.rem(z, 2)
    mate = mate_z * 2 + y
    level = z * 2 + 1 - y
    corner = mate_z * 2 + 1 - y
    near = (mate, level, corner)
    inner = jnp.logical_or(z == 1, z == 2)
    outer = jnp.logical_not(inner)
    far_inner_z = 3 - z
    far_outer_z = lax.rem(z + 2, 4)
    far = (
        far_inner_z * 2 + 1 - y,
        far_outer_z * 2 + 1 - y,
        far_inner_z * 2 + y,
        far_outer_z * 2 + y,
    )
    sections = 4
    sibling = here + 1 - 2 * lax.rem(here, 2)
    across = lax.rem(here + 2, sections)
    other = lax.rem(sibling + 2, sections)
    slab_rows, quarter = master.shape
    blocks = grad.shape[0]
    chunks = quarter // LANES
    slots = capacity * BLOCK

    loads = [
        pltpu.make_async_copy(source, target, load_sem.at[i])
        for i, (source, target) in enumerate(
            [
                (grad_hbm, grad),
                (dlogits_hbm, dlogits),
                (hidden_hbm, hidden),
                (master_hbm, master),
                (moment1_hbm, moment1),
                (moment2_hbm, moment2),
            ]
        )
    ]
    for load in loads:
        load.start()

    barrier = pltpu.get_barrier_semaphore()

    @pl.loop(1, owners)
    def _(d):
        pl.semaphore_signal(
            barrier, inc=1, device_id={"vocab": lax.rem(me + d, owners)}, device_id_type=MESH
        )

    @pl.loop(1, sections)
    def _(e):
        pl.semaphore_signal(
            barrier, inc=1, device_id={"section": lax.rem(here + e, sections)}, device_id_type=MESH
        )

    def send(source, target, sems, where, c=None):
        return pltpu.make_async_remote_copy(
            src_ref=source,
            dst_ref=target,
            send_sem=sems.at[0] if c is None else sems.at[0, c],
            recv_sem=sems.at[1] if c is None else sems.at[1, c],
            device_id=where,
            device_id_type=MESH,
        ).start()

    def await_bytes(ref, sem):
        pltpu.make_async_copy(ref, ref, sem).wait()

    def add_start(o, so_far):
        starts[o] = so_far
        return so_far + counts_ref[0, o]

    lax.fori_loop(0, owners, add_start, jnp.int32(0))

    def pick(owner, slot):
        live = slot < counts_ref[0, owner]
        return live, jnp.where(live, starts[owner] + slot, 0)

    for b in range(blocks):
        owner = lax.fori_loop(
            0,
            owners,
            lambda o, n: n + jnp.where(starts[o] + counts_ref[0, o] <= b, 1, 0),
            jnp.int32(0),
        )
        ids = ids_ref[b : b + 1, :]
        slab_ids[b : b + 1, :] = jnp.where(ids >= 0, ids + owner * slab_rows, -1)

    for i, owner in enumerate(near):
        id_send[i, 0:blocks, :] = slab_ids[...]
        id_send[i, blocks:, :] = jnp.full((8, BLOCK), -1, jnp.int32)
        for slot in range(capacity):
            live, block = pick(owner, slot)
            row = blocks + slot
            id_send[i, row : row + 1, :] = jnp.where(live, ids_ref[pl.ds(block, 1), :], -1)

    pl.semaphore_wait(barrier, owners - 1 + sections - 1)

    for i, owner in enumerate(near):
        send(id_send.at[i], id_got.at[i], id_sems, {"vocab": owner})

    loads[0].wait()

    def columns(c):
        return pl.ds(pl.multiple_of(c * LANES, LANES), LANES)

    def send_slot(i, c):
        for slot in range(capacity):
            _, block = pick(near[i], slot)
            slot_send[c, i, slot * BLOCK : (slot + 1) * BLOCK, :] = grad[block, :, columns(c)]
        send(slot_send.at[c, i], slot_got.at[c, i], slot_sems, {"vocab": near[i]}, c)

    @pl.loop(0, chunks)
    def _(c):
        @pl.when(outer)
        def _():
            send(grad.at[:, :, columns(c)], raw_got.at[c], raw_sems, {"vocab": mate}, c)

        @pl.when(inner)
        def _():
            send_slot(0, c)

        send_slot(1, c)
        send_slot(2, c)

    loads[1].wait()
    loads[2].wait()

    def head_part(section, c):
        at = pl.multiple_of(section * quarter + c * LANES, LANES)
        return jnp.dot(
            dlogits[...], hidden[:, pl.ds(at, LANES)], preferred_element_type=jnp.float32
        )

    @pl.loop(0, chunks)
    def _(c):
        pair_send[c, 0] = head_part(sibling, c).astype(jnp.bfloat16)
        pair_send[c, 1] = head_part(other, c).astype(jnp.bfloat16)
        send(pair_send.at[c], pair_got.at[c], pair_sems, {"section": sibling}, c)

    def one_hot(ids, base):
        rows = lax.broadcasted_iota(jnp.int32, (slab_rows, BLOCK), 0) + base
        return jnp.where(rows == ids, 1.0, 0.0).astype(jnp.bfloat16)

    await_bytes(id_got, id_sems.at[1])

    def block_lanes(b):
        return pl.ds(pl.multiple_of(b * BLOCK, BLOCK), BLOCK)

    @pl.when(inner)
    def _():
        @pl.loop(0, blocks)
        def _(b):
            own_ids = slab_ids[pl.ds(b, 1), :]
            mate_ids = id_got[0, pl.ds(b, 1), :]
            raw_hot[:, block_lanes(b)] = one_hot(mate_ids, me * slab_rows)
            for f in range(4):
                far_hot[f, :, block_lanes(b)] = one_hot(own_ids, far[f] * slab_rows)
                far_hot[f, :, block_lanes(blocks + b)] = one_hot(mate_ids, far[f] * slab_rows)

    @pl.loop(0, chunks)
    def _(c):
        own_part[c] = head_part(here, c)
        mine = head_part(across, c)
        await_bytes(pair_got.at[c], pair_sems.at[1, c])
        cross_send[c] = (mine + pair_got[c, 1].astype(jnp.float32)).astype(jnp.bfloat16)
        send(cross_send.at[c], cross_got.at[c], cross_sems, {"section": across}, c)

    @pl.loop(0, blocks)
    def _(b):
        own_hot[:, block_lanes(b)] = one_hot(slab_ids[pl.ds(b, 1), :], me * slab_rows)

    for i in range(3):
        for slot in range(capacity):
            at = (i * capacity + slot) * BLOCK
            row = blocks + slot
            slot_hot[:, at : at + BLOCK] = one_hot(id_got[i, row : row + 1, :], 0)

    for load in loads[3:]:
        load.wait()

    def dot(a, b):
        return jnp.dot(a, b, preferred_element_type=jnp.float32)

    def own_rows(c):
        return grad[:, :, columns(c)].reshape(blocks * BLOCK, LANES)

    def raw_rows(c):
        return raw_got[c].reshape(blocks * BLOCK, LANES)

    half = blocks * BLOCK

    def far_sum(f, c):
        return dot(far_hot[f, :, 0:half], own_rows(c)) + dot(far_hot[f, :, half:], raw_rows(c))

    def gather_far(c):
        await_bytes(raw_got.at[c], raw_sems.at[1, c])
        for f in range(2):
            relay_send[c, f] = far_sum(f, c).astype(jnp.bfloat16)
        send(relay_send.at[c], relay_got.at[c], relay_sems, {"vocab": level}, c)
        for f in range(2):
            far_keep[lax.rem(c, 2), f] = far_sum(2 + f, c)

    def send_far(c):
        await_bytes(relay_got.at[c], relay_sems.at[1, c])
        for f in range(2):
            far_send[c, f] = (
                far_keep[lax.rem(c, 2), f] + relay_got[c, f].astype(jnp.float32)
            ).astype(jnp.bfloat16)
            send(far_send.at[c, f], far_got.at[c], far_sems, {"vocab": far[2 + f]}, c)

    def update(c):
        cols = columns(c)
        await_bytes(far_got.at[c], far_sems.at[1, c])
        await_bytes(cross_got.at[c], cross_sems.at[1, c])

        @pl.when(inner)
        def _():
            await_bytes(slot_got.at[c, pl.ds(1, 2)], slot_sems.at[1, c])
            total[...] = (
                dot(own_hot[...], own_rows(c))
                + dot(raw_hot[...], raw_rows(c))
                + dot(slot_hot[:, slots:], slot_got[c, 1:3].reshape(2 * slots, LANES))
            )

        @pl.when(outer)
        def _():
            await_bytes(slot_got.at[c], slot_sems.at[1, c])
            total[...] = dot(own_hot[...], own_rows(c)) + dot(
                slot_hot[...], slot_got[c].reshape(3 * slots, LANES)
            )

        gradient = (
            total[...]
            + far_got[c].astype(jnp.float32)
            + own_part[c]
            + pair_got[c, 0].astype(jnp.float32)
            + cross_got[c].astype(jnp.float32)
        )
        new_moment1 = beta_first * moment1[:, cols] + (1.0 - beta_first) * gradient
        new_moment2 = beta_second * moment2[:, cols] + (1.0 - beta_second) * gradient * gradient
        new_master = master[:, cols] - learn_rate * (new_moment1 / first_fix) / (
            jnp.sqrt(new_moment2 / second_fix) + adam_epsilon
        )
        fresh[c] = new_master.astype(jnp.bfloat16)
        send(fresh.at[c], fresh_got.at[c, 1], over_sems, {"section": across}, c)
        send(fresh.at[c], fresh_got.at[c, 0], side_sems, {"section": sibling}, c)
        moment1[:, cols] = new_moment1
        moment2[:, cols] = new_moment2
        master[:, cols] = new_master
        pltpu.make_async_copy(master.at[:, cols], master_out.at[:, cols], store_sem.at[0]).start()
        pltpu.make_async_copy(moment1.at[:, cols], moment1_out.at[:, cols], store_sem.at[1]).start()
        pltpu.make_async_copy(moment2.at[:, cols], moment2_out.at[:, cols], store_sem.at[2]).start()
        store_fresh(fresh.at[c], here, c)

    def store_fresh(source, section, c):
        at = pl.multiple_of(section * quarter + c * LANES, LANES)
        pltpu.make_async_copy(
            source, refreshed_out.at[:, pl.ds(at, LANES)], store_sem.at[3]
        ).start()

    def forward(c):
        await_bytes(fresh_got.at[c, 1], over_sems.at[1, c])
        send(fresh_got.at[c, 1], fresh_got.at[c, 2], forward_sems, {"section": sibling}, c)
        store_fresh(fresh_got.at[c, 1], across, c)
        await_bytes(fresh_got.at[c, 0], side_sems.at[1, c])
        store_fresh(fresh_got.at[c, 0], sibling, c)

    def finish(c):
        await_bytes(fresh_got.at[c, 2], forward_sems.at[1, c])
        store_fresh(fresh_got.at[c, 2], other, c)

    @pl.loop(0, chunks + 6)
    def _(t):
        @pl.when(jnp.logical_and(inner, t < chunks))
        def _():
            gather_far(t)

        @pl.when(jnp.logical_and(inner, jnp.logical_and(t >= 1, t < chunks + 1)))
        def _():
            send_far(t - 1)

        @pl.when(jnp.logical_and(t >= 3, t < chunks + 3))
        def _():
            update(t - 3)

        @pl.when(jnp.logical_and(t >= 5, t < chunks + 5))
        def _():
            forward(t - 5)

        @pl.when(t >= 6)
        def _():
            finish(t - 6)

    await_bytes(id_send, id_sems.at[0])

    @pl.loop(0, chunks)
    def _(c):
        @pl.when(outer)
        def _():
            await_bytes(raw_got.at[c], raw_sems.at[0, c])
            await_bytes(slot_send.at[c, pl.ds(1, 2)], slot_sems.at[0, c])

        @pl.when(inner)
        def _():
            await_bytes(slot_send.at[c], slot_sems.at[0, c])
            await_bytes(relay_send.at[c], relay_sems.at[0, c])
            await_bytes(far_send.at[c], far_sems.at[0, c])

        await_bytes(pair_send.at[c], pair_sems.at[0, c])
        await_bytes(cross_send.at[c], cross_sems.at[0, c])
        await_bytes(fresh.at[c], side_sems.at[0, c])
        await_bytes(fresh.at[c], over_sems.at[0, c])
        await_bytes(fresh.at[c], forward_sems.at[0, c])

    pltpu.make_async_copy(master, master_out, store_sem.at[0]).wait()
    pltpu.make_async_copy(moment1, moment1_out, store_sem.at[1]).wait()
    pltpu.make_async_copy(moment2, moment2_out, store_sem.at[2]).wait()
    pltpu.make_async_copy(refreshed_out, refreshed_out, store_sem.at[3]).wait()


def relay_shards(token_grad, token_ids, block_counts, hidden, dlogits, master, moment1, moment2):
    owners = lax.axis_size("vocab")
    row_total, quarter = token_grad.shape
    blocks = row_total // BLOCK
    capacity = max(1, 2 * blocks // owners)
    slab_rows = master.shape[0]
    tokens, width = hidden.shape
    chunks = quarter // LANES
    slots = capacity * BLOCK
    f32, bf16, i32 = jnp.float32, jnp.bfloat16, jnp.int32
    hbm = pl.BlockSpec(memory_space=pl.ANY)
    dma = pltpu.SemaphoreType.DMA
    slab = (slab_rows, quarter)
    piece = (slab_rows, LANES)
    return pl.pallas_call(
        functools.partial(relay_kernel, capacity),
        out_shape=(
            jax.ShapeDtypeStruct(slab, f32),
            jax.ShapeDtypeStruct(slab, f32),
            jax.ShapeDtypeStruct(slab, f32),
            jax.ShapeDtypeStruct((slab_rows, width), bf16),
        ),
        in_specs=[
            pl.BlockSpec(memory_space=pltpu.SMEM),
            pl.BlockSpec(memory_space=pltpu.VMEM),
            hbm, hbm, hbm, hbm, hbm, hbm,
        ],
        out_specs=(hbm, hbm, hbm, hbm),
        scratch_shapes=[
            pltpu.SMEM((owners,), i32),
            pltpu.VMEM((blocks, BLOCK, quarter), bf16),
            pltpu.VMEM((tokens, width), bf16),
            pltpu.VMEM((slab_rows, tokens), bf16),
            pltpu.VMEM(slab, f32),
            pltpu.VMEM(slab, f32),
            pltpu.VMEM(slab, f32),
            pltpu.VMEM((blocks, BLOCK), i32),
            pltpu.VMEM((3, blocks + 8, BLOCK), i32),
            pltpu.VMEM((3, blocks + 8, BLOCK), i32),
            pltpu.VMEM((chunks, 3, slots, LANES), bf16),
            pltpu.VMEM((chunks, 3, slots, LANES), bf16),
            pltpu.VMEM((chunks, blocks, BLOCK, LANES), bf16),
            pltpu.VMEM((slab_rows, row_total), bf16),
            pltpu.VMEM((slab_rows, row_total), bf16),
            pltpu.VMEM((slab_rows, 3 * slots), bf16),
            pltpu.VMEM((4, slab_rows, 2 * row_total), bf16),
            pltpu.VMEM(piece, f32),
            pltpu.VMEM((2, 2) + piece, f32),
            pltpu.VMEM((chunks, 2) + piece, bf16),
            pltpu.VMEM((chunks, 2) + piece, bf16),
            pltpu.VMEM((chunks, 2) + piece, bf16),
            pltpu.VMEM((chunks,) + piece, bf16),
            pltpu.VMEM((chunks, 2) + piece, bf16),
            pltpu.VMEM((chunks, 2) + piece, bf16),
            pltpu.VMEM((chunks,) + piece, bf16),
            pltpu.VMEM((chunks,) + piece, bf16),
            pltpu.VMEM((chunks,) + piece, f32),
            pltpu.VMEM((chunks,) + piece, bf16),
            pltpu.VMEM((chunks, 3) + piece, bf16),
            dma((6,)),
            dma((4,)),
            dma((2,)),
        ]
        + [dma((2, chunks)) for _ in range(9)],
        compiler_params=pltpu.CompilerParams(
            collective_id=1, has_side_effects=True, vmem_limit_bytes=58 * 1024 * 1024
        ),
    )(
        block_counts,
        token_ids.reshape(blocks, BLOCK),
        token_grad.reshape(blocks, BLOCK, quarter),
        hidden,
        dlogits.T,
        master,
        moment1,
        moment2,
    )


def shards(*arrays):
    if lax.axis_size("vocab") == 8 and lax.axis_size("section") == 4:
        return relay_shards(*arrays)
    return direct_shards(*arrays)


def solution(mesh):
    placed = (
        P("vocab", "section"),
        P("vocab"),
        P("vocab", None),
        P("section", None),
        P("section", "vocab"),
        P("vocab", "section"),
        P("vocab", "section"),
        P("vocab", "section"),
    )
    return jax.shard_map(
        shards,
        mesh=mesh,
        in_specs=placed,
        out_specs=(
            P("vocab", "section"),
            P("vocab", "section"),
            P("vocab", "section"),
            P("vocab", None),
        ),
        check_vma=False,
    )
```

```python
import functools

import jax
import jax.numpy as jnp
from jax import lax
from jax.experimental import pallas as pl
from jax.experimental.pallas import tpu as pltpu
from jax.sharding import PartitionSpec as P

BLOCK = 128
LANES = 128
MESH = pl.DeviceIdType.MESH


beta_first = 0.9
beta_second = 0.999
learn_rate = 0.01
adam_epsilon = 1e-08
first_fix = 1.0 - 0.9**10
second_fix = 1.0 - 0.999**10


def direct_kernel(
    owners, sections, capacity,
    counts_ref, ids_ref, grad_hbm, hidden_hbm, dlogits_hbm, master_hbm, moment1_hbm, moment2_hbm,
    master_out, moment1_out, moment2_out, refreshed_out,
    starts, grad, hidden, dlogits, master, moment1, moment2,
    id_send, id_got, row_send, row_got, one_hot, part, part_got, own_part, fresh, fresh_got,
    load_sem, store_sem, id_send_sem, id_recv_sem, row_send_sem, row_recv_sem,
    part_send_sem, part_recv_sem, fresh_send_sem, fresh_recv_sem,
):
    me = lax.axis_index("vocab")
    here = lax.axis_index("section")
    quarter = master.shape[1]
    chunks = quarter // LANES
    slab_rows = master.shape[0]

    loads = [
        pltpu.make_async_copy(source, target, load_sem.at[i])
        for i, (source, target) in enumerate(
            [
                (grad_hbm, grad),
                (dlogits_hbm, dlogits),
                (hidden_hbm, hidden),
                (master_hbm, master),
                (moment1_hbm, moment1),
                (moment2_hbm, moment2),
            ]
        )
    ]
    for load in loads:
        load.start()

    barrier = pltpu.get_barrier_semaphore()

    @pl.loop(1, owners)
    def _(d):
        pl.semaphore_signal(
            barrier, inc=1, device_id={"vocab": lax.rem(me + d, owners)}, device_id_type=MESH
        )

    @pl.loop(1, sections)
    def _(e):
        pl.semaphore_signal(
            barrier, inc=1, device_id={"section": lax.rem(here + e, sections)}, device_id_type=MESH
        )

    def add_start(o, total):
        starts[o] = total
        return total + counts_ref[0, o]

    lax.fori_loop(0, owners, add_start, jnp.int32(0))

    def pick(owner, slot):
        live = slot < counts_ref[0, owner]
        return live, jnp.where(live, starts[owner] + slot, 0)

    def fill_ids(owner, target):
        target[...] = jnp.full((8, BLOCK), -1, jnp.int32)
        for slot in range(capacity):
            live, block = pick(owner, slot)
            target[slot : slot + 1, :] = jnp.where(live, ids_ref[pl.ds(block, 1), :], -1)

    pl.semaphore_wait(barrier, owners - 1 + sections - 1)

    def id_copy(d):
        return pltpu.make_async_remote_copy(
            src_ref=id_send.at[d - 1],
            dst_ref=id_got.at[d - 1],
            send_sem=id_send_sem,
            recv_sem=id_recv_sem,
            device_id={"vocab": lax.rem(me + d, owners)},
            device_id_type=MESH,
        )

    @pl.loop(1, owners)
    def _(d):
        fill_ids(lax.rem(me + d, owners), id_send.at[d - 1])
        id_copy(d).start()

    fill_ids(me, id_got.at[owners - 1])

    loads[0].wait()

    def fill_rows(owner, c, target):
        for slot in range(capacity):
            _, block = pick(owner, slot)
            target[slot * BLOCK : (slot + 1) * BLOCK, :] = grad[
                block, :, pl.ds(pl.multiple_of(c * LANES, LANES), LANES)
            ]

    @pl.loop(0, chunks)
    def _(c):
        @pl.loop(1, owners)
        def _(d):
            owner = lax.rem(me + d, owners)
            fill_rows(owner, c, row_send.at[c, d - 1])
            pltpu.make_async_remote_copy(
                src_ref=row_send.at[c, d - 1],
                dst_ref=row_got.at[c, d - 1],
                send_sem=row_send_sem.at[c],
                recv_sem=row_recv_sem.at[c],
                device_id={"vocab": owner},
                device_id_type=MESH,
            ).start()

        fill_rows(me, c, row_got.at[c, owners - 1])

    loads[1].wait()
    loads[2].wait()

    def head_part(section, c):
        at = pl.multiple_of(section * quarter + c * LANES, LANES)
        return jnp.dot(
            dlogits[...], hidden[:, pl.ds(at, LANES)], preferred_element_type=jnp.float32
        )

    @pl.loop(0, chunks)
    def _(c):
        @pl.loop(1, sections)
        def _(e):
            section = lax.rem(here + e, sections)
            part[c, e - 1] = head_part(section, c).astype(jnp.bfloat16)
            pltpu.make_async_remote_copy(
                src_ref=part.at[c, e - 1],
                dst_ref=part_got.at[c, e - 1],
                send_sem=part_send_sem.at[c],
                recv_sem=part_recv_sem.at[c],
                device_id={"section": section},
                device_id_type=MESH,
            ).start()

        own_part[c] = head_part(here, c)

    arrived = id_got.at[pl.ds(0, owners - 1)]
    pltpu.make_async_copy(arrived, arrived, id_recv_sem).wait()

    @pl.loop(0, owners)
    def _(s):
        for slot in range(capacity):
            ids = id_got[s, slot : slot + 1, :]
            rows = lax.broadcasted_iota(jnp.int32, (slab_rows, BLOCK), 0)
            at = pl.multiple_of((s * capacity + slot) * BLOCK, BLOCK)
            one_hot[:, pl.ds(at, BLOCK)] = jnp.where(rows == ids, 1.0, 0.0).astype(jnp.bfloat16)

    for load in loads[3:]:
        load.wait()

    @pl.loop(0, chunks)
    def _(c):
        cols = pl.ds(pl.multiple_of(c * LANES, LANES), LANES)
        rows_in = row_got.at[c, pl.ds(0, owners - 1)]
        pltpu.make_async_copy(rows_in, rows_in, row_recv_sem.at[c]).wait()
        parts_in = part_got.at[c]
        pltpu.make_async_copy(parts_in, parts_in, part_recv_sem.at[c]).wait()
        gradient = jnp.dot(
            one_hot[...],
            row_got[c].reshape(owners * capacity * BLOCK, LANES),
            preferred_element_type=jnp.float32,
        )
        head = own_part[c]
        for e in range(sections - 1):
            head = head + part_got[c, e].astype(jnp.float32)
        gradient = gradient + head
        new_moment1 = beta_first * moment1[:, cols] + (1.0 - beta_first) * gradient
        new_moment2 = beta_second * moment2[:, cols] + (1.0 - beta_second) * gradient * gradient
        new_master = master[:, cols] - learn_rate * (new_moment1 / first_fix) / (
            jnp.sqrt(new_moment2 / second_fix) + adam_epsilon
        )
        fresh[c] = new_master.astype(jnp.bfloat16)

        @pl.loop(1, sections)
        def _(e):
            pltpu.make_async_remote_copy(
                src_ref=fresh.at[c],
                dst_ref=fresh_got.at[c, e - 1],
                send_sem=fresh_send_sem.at[c],
                recv_sem=fresh_recv_sem.at[c],
                device_id={"section": lax.rem(here + e, sections)},
                device_id_type=MESH,
            ).start()

        moment1[:, cols] = new_moment1
        moment2[:, cols] = new_moment2
        master[:, cols] = new_master
        pltpu.make_async_copy(master.at[:, cols], master_out.at[:, cols], store_sem.at[0]).start()
        pltpu.make_async_copy(moment1.at[:, cols], moment1_out.at[:, cols], store_sem.at[1]).start()
        pltpu.make_async_copy(moment2.at[:, cols], moment2_out.at[:, cols], store_sem.at[2]).start()
        at = pl.multiple_of(here * quarter + c * LANES, LANES)
        pltpu.make_async_copy(
            fresh.at[c], refreshed_out.at[:, pl.ds(at, LANES)], store_sem.at[3]
        ).start()

    @pl.loop(0, chunks)
    def _(c):
        fresh_in = fresh_got.at[c]
        pltpu.make_async_copy(fresh_in, fresh_in, fresh_recv_sem.at[c]).wait()

        @pl.loop(1, sections)
        def _(e):
            source = lax.rem(here + sections - e, sections)
            at = pl.multiple_of(source * quarter + c * LANES, LANES)
            pltpu.make_async_copy(
                fresh_got.at[c, e - 1], refreshed_out.at[:, pl.ds(at, LANES)], store_sem.at[3]
            ).start()

    pltpu.make_async_copy(id_send, id_send, id_send_sem).wait()

    @pl.loop(0, chunks)
    def _(c):
        pltpu.make_async_copy(row_send.at[c], row_send.at[c], row_send_sem.at[c]).wait()
        pltpu.make_async_copy(part.at[c], part.at[c], part_send_sem.at[c]).wait()
        pltpu.make_async_copy(fresh_got.at[c], fresh_got.at[c], fresh_send_sem.at[c]).wait()

    pltpu.make_async_copy(master, master_out, store_sem.at[0]).wait()
    pltpu.make_async_copy(moment1, moment1_out, store_sem.at[1]).wait()
    pltpu.make_async_copy(moment2, moment2_out, store_sem.at[2]).wait()
    pltpu.make_async_copy(refreshed_out, refreshed_out, store_sem.at[3]).wait()


def direct_shards(token_grad, token_ids, block_counts, hidden, dlogits, master, moment1, moment2):
    owners = lax.axis_size("vocab")
    sections = lax.axis_size("section")
    row_total, quarter = token_grad.shape
    block_total = row_total // BLOCK
    capacity = max(1, 2 * block_total // owners)
    slab_rows = master.shape[0]
    tokens, width = hidden.shape
    chunks = quarter // LANES
    slots = capacity * BLOCK
    f32, bf16 = jnp.float32, jnp.bfloat16
    hbm = pl.BlockSpec(memory_space=pl.ANY)
    dma = pltpu.SemaphoreType.DMA
    slab = (slab_rows, quarter)
    return pl.pallas_call(
        functools.partial(direct_kernel, owners, sections, capacity),
        out_shape=(
            jax.ShapeDtypeStruct(slab, f32),
            jax.ShapeDtypeStruct(slab, f32),
            jax.ShapeDtypeStruct(slab, f32),
            jax.ShapeDtypeStruct((slab_rows, width), bf16),
        ),
        in_specs=[
            pl.BlockSpec(memory_space=pltpu.SMEM),
            pl.BlockSpec(memory_space=pltpu.VMEM),
            hbm, hbm, hbm, hbm, hbm, hbm,
        ],
        out_specs=(hbm, hbm, hbm, hbm),
        scratch_shapes=[
            pltpu.SMEM((owners,), jnp.int32),
            pltpu.VMEM((block_total, BLOCK, quarter), bf16),
            pltpu.VMEM((tokens, width), bf16),
            pltpu.VMEM((slab_rows, tokens), bf16),
            pltpu.VMEM(slab, f32),
            pltpu.VMEM(slab, f32),
            pltpu.VMEM(slab, f32),
            pltpu.VMEM((owners - 1, 8, BLOCK), jnp.int32),
            pltpu.VMEM((owners, 8, BLOCK), jnp.int32),
            pltpu.VMEM((chunks, owners - 1, slots, LANES), bf16),
            pltpu.VMEM((chunks, owners, slots, LANES), bf16),
            pltpu.VMEM((slab_rows, owners * slots), bf16),
            pltpu.VMEM((chunks, sections - 1, slab_rows, LANES), bf16),
            pltpu.VMEM((chunks, sections - 1, slab_rows, LANES), bf16),
            pltpu.VMEM((chunks, slab_rows, LANES), f32),
            pltpu.VMEM((chunks, slab_rows, LANES), bf16),
            pltpu.VMEM((chunks, sections - 1, slab_rows, LANES), bf16),
            dma((6,)),
            dma((4,)),
            dma,
            dma,
            dma((chunks,)),
            dma((chunks,)),
            dma((chunks,)),
            dma((chunks,)),
            dma((chunks,)),
            dma((chunks,)),
        ],
        compiler_params=pltpu.CompilerParams(
            collective_id=0, has_side_effects=True, vmem_limit_bytes=58 * 1024 * 1024
        ),
    )(
        block_counts,
        token_ids.reshape(block_total, BLOCK),
        token_grad.reshape(block_total, BLOCK, quarter),
        hidden,
        dlogits.T,
        master,
        moment1,
        moment2,
    )


def relay_kernel(
    capacity,
    counts_ref, ids_ref, grad_hbm, hidden_hbm, dlogits_hbm, master_hbm, moment1_hbm, moment2_hbm,
    master_out, moment1_out, moment2_out, refreshed_out,
    starts, grad, hidden, dlogits, master, moment1, moment2,
    mate_counts, mate_starts, count_send, count_got, id_send, id_got, slot_send, slot_got, raw_got,
    raw_now, near_raw, near_hot, far_hot, total, far_keep, relay_send, relay_got, far_send, far_got,
    pair_send, pair_got, cross_send, cross_got, own_part, fresh, fresh_got,
    load_sem, store_sem, count_sems, id_sems, slot_sems, raw_sems, relay_sems, far_sems,
    pair_sems, cross_sems, side_sems, over_sems, forward_sems,
):
    owners = counts_ref.shape[1]
    me = lax.axis_index("vocab")
    here = lax.axis_index("section")
    z, y = me // 2, lax.rem(me, 2)
    mate_z = z + 1 - 2 * lax.rem(z, 2)
    mate = mate_z * 2 + y
    level = z * 2 + 1 - y
    corner = mate_z * 2 + 1 - y
    near = (mate, level, corner)
    inner = jnp.logical_or(z == 1, z == 2)
    outer = jnp.logical_not(inner)
    far_inner_z = 3 - z
    far_outer_z = lax.rem(z + 2, 4)
    far = (
        far_inner_z * 2 + 1 - y,
        far_outer_z * 2 + 1 - y,
        far_inner_z * 2 + y,
        far_outer_z * 2 + y,
    )
    sections = 4
    sibling = here + 1 - 2 * lax.rem(here, 2)
    across = lax.rem(here + 2, sections)
    other = lax.rem(sibling + 2, sections)
    slab_rows, quarter = master.shape
    blocks = grad.shape[0]
    chunks = quarter // LANES
    slots = capacity * BLOCK

    loads = [
        pltpu.make_async_copy(source, target, load_sem.at[i])
        for i, (source, target) in enumerate(
            [
                (grad_hbm, grad),
                (dlogits_hbm, dlogits),
                (hidden_hbm, hidden),
                (master_hbm, master),
                (moment1_hbm, moment1),
                (moment2_hbm, moment2),
            ]
        )
    ]
    for load in loads:
        load.start()

    barrier = pltpu.get_barrier_semaphore()

    @pl.loop(1, owners)
    def _(d):
        pl.semaphore_signal(
            barrier, inc=1, device_id={"vocab": lax.rem(me + d, owners)}, device_id_type=MESH
        )

    @pl.loop(1, sections)
    def _(e):
        pl.semaphore_signal(
            barrier, inc=1, device_id={"section": lax.rem(here + e, sections)}, device_id_type=MESH
        )

    def send(source, target, sems, where, c=None):
        return pltpu.make_async_remote_copy(
            src_ref=source,
            dst_ref=target,
            send_sem=sems.at[0] if c is None else sems.at[0, c],
            recv_sem=sems.at[1] if c is None else sems.at[1, c],
            device_id=where,
            device_id_type=MESH,
        ).start()

    def await_bytes(ref, sem):
        pltpu.make_async_copy(ref, ref, sem).wait()

    def sum_starts(target, counts):
        def add_start(o, so_far):
            target[o] = so_far
            return so_far + counts[0, o]

        lax.fori_loop(0, owners, add_start, jnp.int32(0))

    def pick_from(counts, first, owner, slot):
        live = slot < counts[0, owner]
        return live, jnp.where(live, first[owner] + slot, 0)

    def pick(owner, slot):
        return pick_from(counts_ref, starts, owner, slot)

    def mate_pick(owner, slot):
        return pick_from(mate_counts, mate_starts, owner, slot)

    sum_starts(starts, counts_ref)

    def own_ids(owner, slot):
        live, block = pick(owner, slot)
        return jnp.where(live, ids_ref[pl.ds(block, 1), :], -1)

    lanes = lax.broadcasted_iota(jnp.int32, (8, BLOCK), 1)
    count_row = jnp.zeros((8, BLOCK), jnp.int32)
    for o in range(owners):
        count_row = jnp.where(lanes == o, counts_ref[0, o], count_row)
    count_send[...] = count_row

    for i, owner in enumerate(near):
        id_send[i, 0:blocks, :] = ids_ref[...]
        id_send[i, blocks:, :] = jnp.full((8, BLOCK), -1, jnp.int32)
        for slot in range(capacity):
            row = blocks + slot
            id_send[i, row : row + 1, :] = own_ids(owner, slot)

    pl.semaphore_wait(barrier, owners - 1 + sections - 1)

    for i, owner in enumerate(near):
        send(id_send.at[i], id_got.at[i], id_sems, {"vocab": owner})

    send(count_send, count_got, count_sems, {"vocab": mate})

    loads[0].wait()

    def columns(c):
        return pl.ds(pl.multiple_of(c * LANES, LANES), LANES)

    def send_slot(i, c):
        for slot in range(capacity):
            _, block = pick(near[i], slot)
            slot_send[c, i, slot * BLOCK : (slot + 1) * BLOCK, :] = grad[block, :, columns(c)]
        send(slot_send.at[c, i], slot_got.at[c, i], slot_sems, {"vocab": near[i]}, c)

    @pl.when(outer)
    def _():
        @pl.loop(0, chunks)
        def _(c):
            send(grad.at[:, :, columns(c)], raw_got.at[c], raw_sems, {"vocab": mate}, c)

    def send_slots(c):
        @pl.when(inner)
        def _():
            send_slot(0, c)

        send_slot(1, c)
        send_slot(2, c)

    loads[1].wait()
    loads[2].wait()

    def head_part(section, c):
        at = pl.multiple_of(section * quarter + c * LANES, LANES)
        return jnp.dot(
            dlogits[...], hidden[:, pl.ds(at, LANES)], preferred_element_type=jnp.float32
        )

    @pl.loop(0, chunks)
    def _(c):
        pair_send[c, 0] = head_part(sibling, c).astype(jnp.bfloat16)
        pair_send[c, 1] = head_part(other, c).astype(jnp.bfloat16)
        send(pair_send.at[c], pair_got.at[c], pair_sems, {"section": sibling}, c)

    def one_hot(ids):
        rows = lax.broadcasted_iota(jnp.int32, (slab_rows, BLOCK), 0)
        return jnp.where(rows == ids, 1.0, 0.0).astype(jnp.bfloat16)

    await_bytes(id_got, id_sems.at[1])
    await_bytes(count_got, count_sems.at[1])

    @pl.when(inner)
    def _():
        to_scalars = pltpu.make_async_copy(count_got, mate_counts, load_sem.at[6])
        to_scalars.start()
        to_scalars.wait()
        sum_starts(mate_starts, mate_counts)
        for f in range(4):
            for slot in range(capacity):
                at = slot * BLOCK
                far_hot[f, :, at : at + BLOCK] = one_hot(own_ids(far[f], slot))
                live, block = mate_pick(far[f], slot)
                ids = jnp.where(live, id_got[0, pl.ds(block, 1), :], -1)
                at = slots + slot * BLOCK
                far_hot[f, :, at : at + BLOCK] = one_hot(ids)

    @pl.loop(0, chunks)
    def _(c):
        own_part[c] = head_part(here, c)
        mine = head_part(across, c)
        await_bytes(pair_got.at[c], pair_sems.at[1, c])
        cross_send[c] = (mine + pair_got[c, 1].astype(jnp.float32)).astype(jnp.bfloat16)
        send(cross_send.at[c], cross_got.at[c], cross_sems, {"section": across}, c)

    for slot in range(capacity):
        at = slot * BLOCK
        near_hot[:, at : at + BLOCK] = one_hot(own_ids(me, slot))
        for i in range(3):
            at = ((i + 1) * capacity + slot) * BLOCK
            row = blocks + slot
            near_hot[:, at : at + BLOCK] = one_hot(id_got[i, row : row + 1, :])

    for load in loads[3:]:
        load.wait()

    def dot(a, b):
        return jnp.dot(a, b, preferred_element_type=jnp.float32)

    def own_rows(owner, c):
        return [grad[pick(owner, slot)[1], :, columns(c)] for slot in range(capacity)]

    def raw_rows(owner):
        return [raw_now[mate_pick(owner, slot)[1]] for slot in range(capacity)]

    def far_sum(f, c):
        rows = jnp.concatenate(own_rows(far[f], c) + raw_rows(far[f]), axis=0)
        return dot(far_hot[f], rows)

    def gather_far(c):
        await_bytes(raw_got.at[c], raw_sems.at[1, c])
        raw_now[...] = raw_got[c]
        near_raw[lax.rem(c, 4)] = jnp.concatenate(raw_rows(me), axis=0)
        for f in range(2):
            relay_send[c, f] = far_sum(f, c).astype(jnp.bfloat16)
        send(relay_send.at[c], relay_got.at[c], relay_sems, {"vocab": level}, c)
        for f in range(2):
            far_keep[lax.rem(c, 2), f] = far_sum(2 + f, c)

    def send_far(c):
        await_bytes(relay_got.at[c], relay_sems.at[1, c])
        for f in range(2):
            far_send[c, f] = (
                far_keep[lax.rem(c, 2), f] + relay_got[c, f].astype(jnp.float32)
            ).astype(jnp.bfloat16)
            send(far_send.at[c, f], far_got.at[c], far_sems, {"vocab": far[2 + f]}, c)

    def update(c):
        cols = columns(c)
        await_bytes(far_got.at[c], far_sems.at[1, c])
        await_bytes(cross_got.at[c], cross_sems.at[1, c])

        @pl.when(inner)
        def _():
            await_bytes(slot_got.at[c, pl.ds(1, 2)], slot_sems.at[1, c])
            rest = slot_got[c, 1:3].reshape(2 * slots, LANES)
            rows = jnp.concatenate(own_rows(me, c) + [near_raw[lax.rem(c, 4)], rest], axis=0)
            total[...] = dot(near_hot[...], rows)

        @pl.when(outer)
        def _():
            await_bytes(slot_got.at[c], slot_sems.at[1, c])
            rest = slot_got[c].reshape(3 * slots, LANES)
            total[...] = dot(near_hot[...], jnp.concatenate(own_rows(me, c) + [rest], axis=0))

        gradient = (
            total[...]
            + far_got[c].astype(jnp.float32)
            + own_part[c]
            + pair_got[c, 0].astype(jnp.float32)
            + cross_got[c].astype(jnp.float32)
        )
        new_moment1 = beta_first * moment1[:, cols] + (1.0 - beta_first) * gradient
        new_moment2 = beta_second * moment2[:, cols] + (1.0 - beta_second) * gradient * gradient
        new_master = master[:, cols] - learn_rate * (new_moment1 / first_fix) / (
            jnp.sqrt(new_moment2 / second_fix) + adam_epsilon
        )
        fresh[c] = new_master.astype(jnp.bfloat16)
        send(fresh.at[c], fresh_got.at[c, 1], over_sems, {"section": across}, c)
        send(fresh.at[c], fresh_got.at[c, 0], side_sems, {"section": sibling}, c)
        moment1[:, cols] = new_moment1
        moment2[:, cols] = new_moment2
        master[:, cols] = new_master
        pltpu.make_async_copy(master.at[:, cols], master_out.at[:, cols], store_sem.at[0]).start()
        pltpu.make_async_copy(moment1.at[:, cols], moment1_out.at[:, cols], store_sem.at[1]).start()
        pltpu.make_async_copy(moment2.at[:, cols], moment2_out.at[:, cols], store_sem.at[2]).start()
        store_fresh(fresh.at[c], here, c)

    def store_fresh(source, section, c):
        at = pl.multiple_of(section * quarter + c * LANES, LANES)
        pltpu.make_async_copy(
            source, refreshed_out.at[:, pl.ds(at, LANES)], store_sem.at[3]
        ).start()

    def forward(c):
        await_bytes(fresh_got.at[c, 1], over_sems.at[1, c])
        send(fresh_got.at[c, 1], fresh_got.at[c, 2], forward_sems, {"section": sibling}, c)
        store_fresh(fresh_got.at[c, 1], across, c)
        await_bytes(fresh_got.at[c, 0], side_sems.at[1, c])
        store_fresh(fresh_got.at[c, 0], sibling, c)

    def finish(c):
        await_bytes(fresh_got.at[c, 2], forward_sems.at[1, c])
        store_fresh(fresh_got.at[c, 2], other, c)

    @pl.loop(0, chunks + 6)
    def _(t):
        @pl.when(jnp.logical_and(inner, t < chunks))
        def _():
            gather_far(t)

        @pl.when(t < chunks)
        def _():
            send_slots(t)

        @pl.when(jnp.logical_and(inner, jnp.logical_and(t >= 1, t < chunks + 1)))
        def _():
            send_far(t - 1)

        @pl.when(jnp.logical_and(t >= 3, t < chunks + 3))
        def _():
            update(t - 3)

        @pl.when(jnp.logical_and(t >= 5, t < chunks + 5))
        def _():
            forward(t - 5)

        @pl.when(t >= 6)
        def _():
            finish(t - 6)

    await_bytes(id_send, id_sems.at[0])
    await_bytes(count_send, count_sems.at[0])

    @pl.loop(0, chunks)
    def _(c):
        @pl.when(outer)
        def _():
            await_bytes(raw_got.at[c], raw_sems.at[0, c])
            await_bytes(slot_send.at[c, pl.ds(1, 2)], slot_sems.at[0, c])

        @pl.when(inner)
        def _():
            await_bytes(slot_send.at[c], slot_sems.at[0, c])
            await_bytes(relay_send.at[c], relay_sems.at[0, c])
            await_bytes(far_send.at[c], far_sems.at[0, c])

        await_bytes(pair_send.at[c], pair_sems.at[0, c])
        await_bytes(cross_send.at[c], cross_sems.at[0, c])
        await_bytes(fresh.at[c], side_sems.at[0, c])
        await_bytes(fresh.at[c], over_sems.at[0, c])
        await_bytes(fresh.at[c], forward_sems.at[0, c])

    pltpu.make_async_copy(master, master_out, store_sem.at[0]).wait()
    pltpu.make_async_copy(moment1, moment1_out, store_sem.at[1]).wait()
    pltpu.make_async_copy(moment2, moment2_out, store_sem.at[2]).wait()
    pltpu.make_async_copy(refreshed_out, refreshed_out, store_sem.at[3]).wait()


def relay_shards(token_grad, token_ids, block_counts, hidden, dlogits, master, moment1, moment2):
    owners = lax.axis_size("vocab")
    row_total, quarter = token_grad.shape
    blocks = row_total // BLOCK
    capacity = max(1, 2 * blocks // owners)
    slab_rows = master.shape[0]
    tokens, width = hidden.shape
    chunks = quarter // LANES
    slots = capacity * BLOCK
    f32, bf16, i32 = jnp.float32, jnp.bfloat16, jnp.int32
    hbm = pl.BlockSpec(memory_space=pl.ANY)
    dma = pltpu.SemaphoreType.DMA
    slab = (slab_rows, quarter)
    piece = (slab_rows, LANES)
    return pl.pallas_call(
        functools.partial(relay_kernel, capacity),
        out_shape=(
            jax.ShapeDtypeStruct(slab, f32),
            jax.ShapeDtypeStruct(slab, f32),
            jax.ShapeDtypeStruct(slab, f32),
            jax.ShapeDtypeStruct((slab_rows, width), bf16),
        ),
        in_specs=[
            pl.BlockSpec(memory_space=pltpu.SMEM),
            pl.BlockSpec(memory_space=pltpu.VMEM),
            hbm, hbm, hbm, hbm, hbm, hbm,
        ],
        out_specs=(hbm, hbm, hbm, hbm),
        scratch_shapes=[
            pltpu.SMEM((owners,), i32),
            pltpu.VMEM((blocks, BLOCK, quarter), bf16),
            pltpu.VMEM((tokens, width), bf16),
            pltpu.VMEM((slab_rows, tokens), bf16),
            pltpu.VMEM(slab, f32),
            pltpu.VMEM(slab, f32),
            pltpu.VMEM(slab, f32),
            pltpu.SMEM((8, BLOCK), i32),
            pltpu.SMEM((owners,), i32),
            pltpu.VMEM((8, BLOCK), i32),
            pltpu.VMEM((8, BLOCK), i32),
            pltpu.VMEM((3, blocks + 8, BLOCK), i32),
            pltpu.VMEM((3, blocks + 8, BLOCK), i32),
            pltpu.VMEM((chunks, 3, slots, LANES), bf16),
            pltpu.VMEM((chunks, 3, slots, LANES), bf16),
            pltpu.VMEM((chunks, blocks, BLOCK, LANES), bf16),
            pltpu.VMEM((blocks, BLOCK, LANES), bf16),
            pltpu.VMEM((4, slots, LANES), bf16),
            pltpu.VMEM((slab_rows, 4 * slots), bf16),
            pltpu.VMEM((4, slab_rows, 2 * slots), bf16),
            pltpu.VMEM(piece, f32),
            pltpu.VMEM((2, 2) + piece, f32),
            pltpu.VMEM((chunks, 2) + piece, bf16),
            pltpu.VMEM((chunks, 2) + piece, bf16),
            pltpu.VMEM((chunks, 2) + piece, bf16),
            pltpu.VMEM((chunks,) + piece, bf16),
            pltpu.VMEM((chunks, 2) + piece, bf16),
            pltpu.VMEM((chunks, 2) + piece, bf16),
            pltpu.VMEM((chunks,) + piece, bf16),
            pltpu.VMEM((chunks,) + piece, bf16),
            pltpu.VMEM((chunks,) + piece, f32),
            pltpu.VMEM((chunks,) + piece, bf16),
            pltpu.VMEM((chunks, 3) + piece, bf16),
            dma((7,)),
            dma((4,)),
            dma((2,)),
            dma((2,)),
        ]
        + [dma((2, chunks)) for _ in range(9)],
        compiler_params=pltpu.CompilerParams(
            collective_id=1, has_side_effects=True, vmem_limit_bytes=52 * 1024 * 1024
        ),
    )(
        block_counts,
        token_ids.reshape(blocks, BLOCK),
        token_grad.reshape(blocks, BLOCK, quarter),
        hidden,
        dlogits.T,
        master,
        moment1,
        moment2,
    )


def shards(*arrays):
    if lax.axis_size("vocab") == 8 and lax.axis_size("section") == 4:
        return relay_shards(*arrays)
    return direct_shards(*arrays)


def solution(mesh):
    placed = (
        P("vocab", "section"),
        P("vocab"),
        P("vocab", None),
        P("section", None),
        P("section", "vocab"),
        P("vocab", "section"),
        P("vocab", "section"),
        P("vocab", "section"),
    )
    return jax.shard_map(
        shards,
        mesh=mesh,
        in_specs=placed,
        out_specs=(
            P("vocab", "section"),
            P("vocab", "section"),
            P("vocab", "section"),
            P("vocab", None),
        ),
        check_vma=False,
    )
```

```python
import functools

import jax
import jax.numpy as jnp
from jax import lax
from jax.experimental import pallas as pl
from jax.experimental.pallas import tpu as pltpu
from jax.sharding import PartitionSpec as P

BLOCK = 128
LANES = 128
MESH = pl.DeviceIdType.MESH


beta_first = 0.9
beta_second = 0.999
learn_rate = 0.01
adam_epsilon = 1e-08
first_fix = 1.0 - 0.9**10
second_fix = 1.0 - 0.999**10


def direct_kernel(
    owners, sections, capacity,
    counts_ref, ids_ref, grad_hbm, hidden_hbm, dlogits_hbm, master_hbm, moment1_hbm, moment2_hbm,
    master_out, moment1_out, moment2_out, refreshed_out,
    starts, grad, hidden, dlogits, master, moment1, moment2,
    id_send, id_got, row_send, row_got, one_hot, part, part_got, own_part, fresh, fresh_got,
    load_sem, store_sem, id_send_sem, id_recv_sem, row_send_sem, row_recv_sem,
    part_send_sem, part_recv_sem, fresh_send_sem, fresh_recv_sem,
):
    me = lax.axis_index("vocab")
    here = lax.axis_index("section")
    quarter = master.shape[1]
    chunks = quarter // LANES
    slab_rows = master.shape[0]

    loads = [
        pltpu.make_async_copy(source, target, load_sem.at[i])
        for i, (source, target) in enumerate(
            [
                (grad_hbm, grad),
                (dlogits_hbm, dlogits),
                (hidden_hbm, hidden),
                (master_hbm, master),
                (moment1_hbm, moment1),
                (moment2_hbm, moment2),
            ]
        )
    ]
    for load in loads:
        load.start()

    barrier = pltpu.get_barrier_semaphore()

    @pl.loop(1, owners)
    def _(d):
        pl.semaphore_signal(
            barrier, inc=1, device_id={"vocab": lax.rem(me + d, owners)}, device_id_type=MESH
        )

    @pl.loop(1, sections)
    def _(e):
        pl.semaphore_signal(
            barrier, inc=1, device_id={"section": lax.rem(here + e, sections)}, device_id_type=MESH
        )

    def add_start(o, total):
        starts[o] = total
        return total + counts_ref[0, o]

    lax.fori_loop(0, owners, add_start, jnp.int32(0))

    def pick(owner, slot):
        live = slot < counts_ref[0, owner]
        return live, jnp.where(live, starts[owner] + slot, 0)

    def fill_ids(owner, target):
        target[...] = jnp.full((8, BLOCK), -1, jnp.int32)
        for slot in range(capacity):
            live, block = pick(owner, slot)
            target[slot : slot + 1, :] = jnp.where(live, ids_ref[pl.ds(block, 1), :], -1)

    pl.semaphore_wait(barrier, owners - 1 + sections - 1)

    def id_copy(d):
        return pltpu.make_async_remote_copy(
            src_ref=id_send.at[d - 1],
            dst_ref=id_got.at[d - 1],
            send_sem=id_send_sem,
            recv_sem=id_recv_sem,
            device_id={"vocab": lax.rem(me + d, owners)},
            device_id_type=MESH,
        )

    @pl.loop(1, owners)
    def _(d):
        fill_ids(lax.rem(me + d, owners), id_send.at[d - 1])
        id_copy(d).start()

    fill_ids(me, id_got.at[owners - 1])

    loads[0].wait()

    def fill_rows(owner, c, target):
        for slot in range(capacity):
            _, block = pick(owner, slot)
            target[slot * BLOCK : (slot + 1) * BLOCK, :] = grad[
                block, :, pl.ds(pl.multiple_of(c * LANES, LANES), LANES)
            ]

    @pl.loop(0, chunks)
    def _(c):
        @pl.loop(1, owners)
        def _(d):
            owner = lax.rem(me + d, owners)
            fill_rows(owner, c, row_send.at[c, d - 1])
            pltpu.make_async_remote_copy(
                src_ref=row_send.at[c, d - 1],
                dst_ref=row_got.at[c, d - 1],
                send_sem=row_send_sem.at[c],
                recv_sem=row_recv_sem.at[c],
                device_id={"vocab": owner},
                device_id_type=MESH,
            ).start()

        fill_rows(me, c, row_got.at[c, owners - 1])

    loads[1].wait()
    loads[2].wait()

    def head_part(section, c):
        at = pl.multiple_of(section * quarter + c * LANES, LANES)
        return jnp.dot(
            dlogits[...], hidden[:, pl.ds(at, LANES)], preferred_element_type=jnp.float32
        )

    @pl.loop(0, chunks)
    def _(c):
        @pl.loop(1, sections)
        def _(e):
            section = lax.rem(here + e, sections)
            part[c, e - 1] = head_part(section, c).astype(jnp.bfloat16)
            pltpu.make_async_remote_copy(
                src_ref=part.at[c, e - 1],
                dst_ref=part_got.at[c, e - 1],
                send_sem=part_send_sem.at[c],
                recv_sem=part_recv_sem.at[c],
                device_id={"section": section},
                device_id_type=MESH,
            ).start()

        own_part[c] = head_part(here, c)

    arrived = id_got.at[pl.ds(0, owners - 1)]
    pltpu.make_async_copy(arrived, arrived, id_recv_sem).wait()

    @pl.loop(0, owners)
    def _(s):
        for slot in range(capacity):
            ids = id_got[s, slot : slot + 1, :]
            rows = lax.broadcasted_iota(jnp.int32, (slab_rows, BLOCK), 0)
            at = pl.multiple_of((s * capacity + slot) * BLOCK, BLOCK)
            one_hot[:, pl.ds(at, BLOCK)] = jnp.where(rows == ids, 1.0, 0.0).astype(jnp.bfloat16)

    for load in loads[3:]:
        load.wait()

    @pl.loop(0, chunks)
    def _(c):
        cols = pl.ds(pl.multiple_of(c * LANES, LANES), LANES)
        rows_in = row_got.at[c, pl.ds(0, owners - 1)]
        pltpu.make_async_copy(rows_in, rows_in, row_recv_sem.at[c]).wait()
        parts_in = part_got.at[c]
        pltpu.make_async_copy(parts_in, parts_in, part_recv_sem.at[c]).wait()
        gradient = jnp.dot(
            one_hot[...],
            row_got[c].reshape(owners * capacity * BLOCK, LANES),
            preferred_element_type=jnp.float32,
        )
        head = own_part[c]
        for e in range(sections - 1):
            head = head + part_got[c, e].astype(jnp.float32)
        gradient = gradient + head
        new_moment1 = beta_first * moment1[:, cols] + (1.0 - beta_first) * gradient
        new_moment2 = beta_second * moment2[:, cols] + (1.0 - beta_second) * gradient * gradient
        new_master = master[:, cols] - learn_rate * (new_moment1 / first_fix) / (
            jnp.sqrt(new_moment2 / second_fix) + adam_epsilon
        )
        fresh[c] = new_master.astype(jnp.bfloat16)

        @pl.loop(1, sections)
        def _(e):
            pltpu.make_async_remote_copy(
                src_ref=fresh.at[c],
                dst_ref=fresh_got.at[c, e - 1],
                send_sem=fresh_send_sem.at[c],
                recv_sem=fresh_recv_sem.at[c],
                device_id={"section": lax.rem(here + e, sections)},
                device_id_type=MESH,
            ).start()

        moment1[:, cols] = new_moment1
        moment2[:, cols] = new_moment2
        master[:, cols] = new_master
        pltpu.make_async_copy(master.at[:, cols], master_out.at[:, cols], store_sem.at[0]).start()
        pltpu.make_async_copy(moment1.at[:, cols], moment1_out.at[:, cols], store_sem.at[1]).start()
        pltpu.make_async_copy(moment2.at[:, cols], moment2_out.at[:, cols], store_sem.at[2]).start()
        at = pl.multiple_of(here * quarter + c * LANES, LANES)
        pltpu.make_async_copy(
            fresh.at[c], refreshed_out.at[:, pl.ds(at, LANES)], store_sem.at[3]
        ).start()

    @pl.loop(0, chunks)
    def _(c):
        fresh_in = fresh_got.at[c]
        pltpu.make_async_copy(fresh_in, fresh_in, fresh_recv_sem.at[c]).wait()

        @pl.loop(1, sections)
        def _(e):
            source = lax.rem(here + sections - e, sections)
            at = pl.multiple_of(source * quarter + c * LANES, LANES)
            pltpu.make_async_copy(
                fresh_got.at[c, e - 1], refreshed_out.at[:, pl.ds(at, LANES)], store_sem.at[3]
            ).start()

    pltpu.make_async_copy(id_send, id_send, id_send_sem).wait()

    @pl.loop(0, chunks)
    def _(c):
        pltpu.make_async_copy(row_send.at[c], row_send.at[c], row_send_sem.at[c]).wait()
        pltpu.make_async_copy(part.at[c], part.at[c], part_send_sem.at[c]).wait()
        pltpu.make_async_copy(fresh_got.at[c], fresh_got.at[c], fresh_send_sem.at[c]).wait()

    pltpu.make_async_copy(master, master_out, store_sem.at[0]).wait()
    pltpu.make_async_copy(moment1, moment1_out, store_sem.at[1]).wait()
    pltpu.make_async_copy(moment2, moment2_out, store_sem.at[2]).wait()
    pltpu.make_async_copy(refreshed_out, refreshed_out, store_sem.at[3]).wait()


def direct_shards(token_grad, token_ids, block_counts, hidden, dlogits, master, moment1, moment2):
    owners = lax.axis_size("vocab")
    sections = lax.axis_size("section")
    row_total, quarter = token_grad.shape
    block_total = row_total // BLOCK
    capacity = max(1, 2 * block_total // owners)
    slab_rows = master.shape[0]
    tokens, width = hidden.shape
    chunks = quarter // LANES
    slots = capacity * BLOCK
    f32, bf16 = jnp.float32, jnp.bfloat16
    hbm = pl.BlockSpec(memory_space=pl.ANY)
    dma = pltpu.SemaphoreType.DMA
    slab = (slab_rows, quarter)
    return pl.pallas_call(
        functools.partial(direct_kernel, owners, sections, capacity),
        out_shape=(
            jax.ShapeDtypeStruct(slab, f32),
            jax.ShapeDtypeStruct(slab, f32),
            jax.ShapeDtypeStruct(slab, f32),
            jax.ShapeDtypeStruct((slab_rows, width), bf16),
        ),
        in_specs=[
            pl.BlockSpec(memory_space=pltpu.SMEM),
            pl.BlockSpec(memory_space=pltpu.VMEM),
            hbm, hbm, hbm, hbm, hbm, hbm,
        ],
        out_specs=(hbm, hbm, hbm, hbm),
        scratch_shapes=[
            pltpu.SMEM((owners,), jnp.int32),
            pltpu.VMEM((block_total, BLOCK, quarter), bf16),
            pltpu.VMEM((tokens, width), bf16),
            pltpu.VMEM((slab_rows, tokens), bf16),
            pltpu.VMEM(slab, f32),
            pltpu.VMEM(slab, f32),
            pltpu.VMEM(slab, f32),
            pltpu.VMEM((owners - 1, 8, BLOCK), jnp.int32),
            pltpu.VMEM((owners, 8, BLOCK), jnp.int32),
            pltpu.VMEM((chunks, owners - 1, slots, LANES), bf16),
            pltpu.VMEM((chunks, owners, slots, LANES), bf16),
            pltpu.VMEM((slab_rows, owners * slots), bf16),
            pltpu.VMEM((chunks, sections - 1, slab_rows, LANES), bf16),
            pltpu.VMEM((chunks, sections - 1, slab_rows, LANES), bf16),
            pltpu.VMEM((chunks, slab_rows, LANES), f32),
            pltpu.VMEM((chunks, slab_rows, LANES), bf16),
            pltpu.VMEM((chunks, sections - 1, slab_rows, LANES), bf16),
            dma((6,)),
            dma((4,)),
            dma,
            dma,
            dma((chunks,)),
            dma((chunks,)),
            dma((chunks,)),
            dma((chunks,)),
            dma((chunks,)),
            dma((chunks,)),
        ],
        compiler_params=pltpu.CompilerParams(
            collective_id=0, has_side_effects=True, vmem_limit_bytes=58 * 1024 * 1024
        ),
    )(
        block_counts,
        token_ids.reshape(block_total, BLOCK),
        token_grad.reshape(block_total, BLOCK, quarter),
        hidden,
        dlogits.T,
        master,
        moment1,
        moment2,
    )


def relay_kernel(
    capacity,
    counts_ref, ids_ref, grad_hbm, hidden_hbm, dlogits_hbm, master_hbm, moment1_hbm, moment2_hbm,
    gradient_out, refreshed_out,
    starts, grad, hidden, dlogits, master, moment1, moment2,
    mate_counts, mate_starts, count_send, count_got, id_send, id_got, slot_send, slot_got, raw_got,
    raw_now, near_raw, near_hot, far_hot, total, far_keep, relay_send, relay_got, far_send, far_got,
    pair_send, pair_got, cross_send, cross_got, own_part, fresh, fresh_got,
    load_sem, store_sem, count_sems, id_sems, slot_sems, raw_sems, relay_sems, far_sems,
    pair_sems, cross_sems, side_sems, over_sems, forward_sems,
):
    owners = counts_ref.shape[1]
    me = lax.axis_index("vocab")
    here = lax.axis_index("section")
    z, y = me // 2, lax.rem(me, 2)
    mate_z = z + 1 - 2 * lax.rem(z, 2)
    mate = mate_z * 2 + y
    level = z * 2 + 1 - y
    corner = mate_z * 2 + 1 - y
    near = (mate, level, corner)
    inner = jnp.logical_or(z == 1, z == 2)
    outer = jnp.logical_not(inner)
    far_inner_z = 3 - z
    far_outer_z = lax.rem(z + 2, 4)
    far = (
        far_inner_z * 2 + 1 - y,
        far_outer_z * 2 + 1 - y,
        far_inner_z * 2 + y,
        far_outer_z * 2 + y,
    )
    sections = 4
    sibling = here + 1 - 2 * lax.rem(here, 2)
    across = lax.rem(here + 2, sections)
    other = lax.rem(sibling + 2, sections)
    slab_rows, quarter = master.shape
    blocks = grad.shape[0]
    chunks = quarter // LANES
    slots = capacity * BLOCK

    loads = [
        pltpu.make_async_copy(source, target, load_sem.at[i])
        for i, (source, target) in enumerate(
            [
                (grad_hbm, grad),
                (dlogits_hbm, dlogits),
                (hidden_hbm, hidden),
                (master_hbm, master),
                (moment1_hbm, moment1),
                (moment2_hbm, moment2),
            ]
        )
    ]
    for load in loads:
        load.start()

    barrier = pltpu.get_barrier_semaphore()

    @pl.loop(1, owners)
    def _(d):
        pl.semaphore_signal(
            barrier, inc=1, device_id={"vocab": lax.rem(me + d, owners)}, device_id_type=MESH
        )

    @pl.loop(1, sections)
    def _(e):
        pl.semaphore_signal(
            barrier, inc=1, device_id={"section": lax.rem(here + e, sections)}, device_id_type=MESH
        )

    def send(source, target, sems, where, c=None):
        return pltpu.make_async_remote_copy(
            src_ref=source,
            dst_ref=target,
            send_sem=sems.at[0] if c is None else sems.at[0, c],
            recv_sem=sems.at[1] if c is None else sems.at[1, c],
            device_id=where,
            device_id_type=MESH,
        ).start()

    def await_bytes(ref, sem):
        pltpu.make_async_copy(ref, ref, sem).wait()

    def sum_starts(target, counts):
        def add_start(o, so_far):
            target[o] = so_far
            return so_far + counts[0, o]

        lax.fori_loop(0, owners, add_start, jnp.int32(0))

    def pick_from(counts, first, owner, slot):
        live = slot < counts[0, owner]
        return live, jnp.where(live, first[owner] + slot, 0)

    def pick(owner, slot):
        return pick_from(counts_ref, starts, owner, slot)

    def mate_pick(owner, slot):
        return pick_from(mate_counts, mate_starts, owner, slot)

    sum_starts(starts, counts_ref)

    def own_ids(owner, slot):
        live, block = pick(owner, slot)
        return jnp.where(live, ids_ref[pl.ds(block, 1), :], -1)

    lanes = lax.broadcasted_iota(jnp.int32, (8, BLOCK), 1)
    count_row = jnp.zeros((8, BLOCK), jnp.int32)
    for o in range(owners):
        count_row = jnp.where(lanes == o, counts_ref[0, o], count_row)
    count_send[...] = count_row

    for i, owner in enumerate(near):
        id_send[i, 0:blocks, :] = ids_ref[...]
        id_send[i, blocks:, :] = jnp.full((8, BLOCK), -1, jnp.int32)
        for slot in range(capacity):
            row = blocks + slot
            id_send[i, row : row + 1, :] = own_ids(owner, slot)

    pl.semaphore_wait(barrier, owners - 1 + sections - 1)

    for i, owner in enumerate(near):
        send(id_send.at[i], id_got.at[i], id_sems, {"vocab": owner})

    send(count_send, count_got, count_sems, {"vocab": mate})

    loads[0].wait()

    def columns(c):
        return pl.ds(pl.multiple_of(c * LANES, LANES), LANES)

    def send_slot(i, c):
        for slot in range(capacity):
            _, block = pick(near[i], slot)
            slot_send[c, i, slot * BLOCK : (slot + 1) * BLOCK, :] = grad[block, :, columns(c)]
        send(slot_send.at[c, i], slot_got.at[c, i], slot_sems, {"vocab": near[i]}, c)

    @pl.when(outer)
    def _():
        @pl.loop(0, chunks)
        def _(c):
            send(grad.at[:, :, columns(c)], raw_got.at[c], raw_sems, {"vocab": mate}, c)
            send_slot(1, c)
            send_slot(2, c)

    loads[1].wait()
    loads[2].wait()

    def head_part(section, c):
        at = pl.multiple_of(section * quarter + c * LANES, LANES)
        return jnp.dot(
            dlogits[...], hidden[:, pl.ds(at, LANES)], preferred_element_type=jnp.float32
        )

    @pl.loop(0, chunks)
    def _(c):
        pair_send[c, 0] = head_part(sibling, c).astype(jnp.bfloat16)
        pair_send[c, 1] = head_part(other, c).astype(jnp.bfloat16)
        send(pair_send.at[c], pair_got.at[c], pair_sems, {"section": sibling}, c)

    def one_hot(ids):
        rows = lax.broadcasted_iota(jnp.int32, (slab_rows, BLOCK), 0)
        return jnp.where(rows == ids, 1.0, 0.0).astype(jnp.bfloat16)

    await_bytes(id_got, id_sems.at[1])
    await_bytes(count_got, count_sems.at[1])

    @pl.when(inner)
    def _():
        to_scalars = pltpu.make_async_copy(count_got, mate_counts, load_sem.at[6])
        to_scalars.start()
        to_scalars.wait()
        sum_starts(mate_starts, mate_counts)
        for f in range(4):
            for slot in range(capacity):
                at = slot * BLOCK
                far_hot[f, :, at : at + BLOCK] = one_hot(own_ids(far[f], slot))
                live, block = mate_pick(far[f], slot)
                ids = jnp.where(live, id_got[0, pl.ds(block, 1), :], -1)
                at = slots + slot * BLOCK
                far_hot[f, :, at : at + BLOCK] = one_hot(ids)

    @pl.loop(0, chunks)
    def _(c):
        own_part[c] = head_part(here, c)
        mine = head_part(across, c)
        await_bytes(pair_got.at[c], pair_sems.at[1, c])
        cross_send[c] = (mine + pair_got[c, 1].astype(jnp.float32)).astype(jnp.bfloat16)
        send(cross_send.at[c], cross_got.at[c], cross_sems, {"section": across}, c)

    for slot in range(capacity):
        at = slot * BLOCK
        near_hot[:, at : at + BLOCK] = one_hot(own_ids(me, slot))
        for i in range(3):
            at = ((i + 1) * capacity + slot) * BLOCK
            row = blocks + slot
            near_hot[:, at : at + BLOCK] = one_hot(id_got[i, row : row + 1, :])

    for load in loads[3:]:
        load.wait()

    def dot(a, b):
        return jnp.dot(a, b, preferred_element_type=jnp.float32)

    def own_rows(owner, c):
        return [grad[pick(owner, slot)[1], :, columns(c)] for slot in range(capacity)]

    def raw_rows(owner):
        return [raw_now[mate_pick(owner, slot)[1]] for slot in range(capacity)]

    def far_sum(f, c):
        rows = jnp.concatenate(own_rows(far[f], c) + raw_rows(far[f]), axis=0)
        return dot(far_hot[f], rows)

    def gather_far(c):
        await_bytes(raw_got.at[c], raw_sems.at[1, c])
        raw_now[...] = raw_got[c]
        near_raw[lax.rem(c, 4)] = jnp.concatenate(raw_rows(me), axis=0)
        for f in range(2):
            relay_send[c, f] = far_sum(f, c).astype(jnp.bfloat16)
        send(relay_send.at[c], relay_got.at[c], relay_sems, {"vocab": level}, c)
        for f in range(2):
            far_keep[lax.rem(c, 2), f] = far_sum(2 + f, c)

    def send_far(c):
        await_bytes(relay_got.at[c], relay_sems.at[1, c])
        for f in range(2):
            far_send[c, f] = (
                far_keep[lax.rem(c, 2), f] + relay_got[c, f].astype(jnp.float32)
            ).astype(jnp.bfloat16)
            send(far_send.at[c, f], far_got.at[c], far_sems, {"vocab": far[2 + f]}, c)

    def update(c):
        cols = columns(c)
        await_bytes(far_got.at[c], far_sems.at[1, c])
        await_bytes(cross_got.at[c], cross_sems.at[1, c])

        @pl.when(inner)
        def _():
            await_bytes(slot_got.at[c, pl.ds(1, 2)], slot_sems.at[1, c])
            rest = slot_got[c, 1:3].reshape(2 * slots, LANES)
            rows = jnp.concatenate(own_rows(me, c) + [near_raw[lax.rem(c, 4)], rest], axis=0)
            total[...] = dot(near_hot[...], rows)

        @pl.when(outer)
        def _():
            await_bytes(slot_got.at[c], slot_sems.at[1, c])
            rest = slot_got[c].reshape(3 * slots, LANES)
            total[...] = dot(near_hot[...], jnp.concatenate(own_rows(me, c) + [rest], axis=0))

        gradient = (
            total[...]
            + far_got[c].astype(jnp.float32)
            + own_part[c]
            + pair_got[c, 0].astype(jnp.float32)
            + cross_got[c].astype(jnp.float32)
        )
        new_moment1 = beta_first * moment1[:, cols] + (1.0 - beta_first) * gradient
        new_moment2 = beta_second * moment2[:, cols] + (1.0 - beta_second) * gradient * gradient
        new_master = master[:, cols] - learn_rate * (new_moment1 / first_fix) / (
            jnp.sqrt(new_moment2 / second_fix) + adam_epsilon
        )
        fresh[c] = new_master.astype(jnp.bfloat16)
        send(fresh.at[c], fresh_got.at[c, 1], over_sems, {"section": across}, c)
        send(fresh.at[c], fresh_got.at[c, 0], side_sems, {"section": sibling}, c)
        moment1[:, cols] = gradient
        pltpu.make_async_copy(
            moment1.at[:, cols], gradient_out.at[:, cols], store_sem.at[0]
        ).start()
        store_fresh(fresh.at[c], here, c)

    def store_fresh(source, section, c):
        at = pl.multiple_of(section * quarter + c * LANES, LANES)
        pltpu.make_async_copy(
            source, refreshed_out.at[:, pl.ds(at, LANES)], store_sem.at[3]
        ).start()

    def forward(c):
        await_bytes(fresh_got.at[c, 1], over_sems.at[1, c])
        send(fresh_got.at[c, 1], fresh_got.at[c, 2], forward_sems, {"section": sibling}, c)
        store_fresh(fresh_got.at[c, 1], across, c)
        await_bytes(fresh_got.at[c, 0], side_sems.at[1, c])
        store_fresh(fresh_got.at[c, 0], sibling, c)

    def finish(c):
        await_bytes(fresh_got.at[c, 2], forward_sems.at[1, c])
        store_fresh(fresh_got.at[c, 2], other, c)

    @pl.loop(0, chunks + 6)
    def _(t):
        @pl.when(jnp.logical_and(inner, t < chunks))
        def _():
            gather_far(t)
            for i in range(3):
                send_slot(i, t)

        @pl.when(jnp.logical_and(inner, jnp.logical_and(t >= 1, t < chunks + 1)))
        def _():
            send_far(t - 1)

        @pl.when(jnp.logical_and(t >= 3, t < chunks + 3))
        def _():
            update(t - 3)

        @pl.when(jnp.logical_and(t >= 5, t < chunks + 5))
        def _():
            forward(t - 5)

        @pl.when(t >= 6)
        def _():
            finish(t - 6)

    await_bytes(id_send, id_sems.at[0])
    await_bytes(count_send, count_sems.at[0])

    @pl.loop(0, chunks)
    def _(c):
        @pl.when(outer)
        def _():
            await_bytes(raw_got.at[c], raw_sems.at[0, c])
            await_bytes(slot_send.at[c, pl.ds(1, 2)], slot_sems.at[0, c])

        @pl.when(inner)
        def _():
            await_bytes(slot_send.at[c], slot_sems.at[0, c])
            await_bytes(relay_send.at[c], relay_sems.at[0, c])
            await_bytes(far_send.at[c], far_sems.at[0, c])

        await_bytes(pair_send.at[c], pair_sems.at[0, c])
        await_bytes(cross_send.at[c], cross_sems.at[0, c])
        await_bytes(fresh.at[c], side_sems.at[0, c])
        await_bytes(fresh.at[c], over_sems.at[0, c])
        await_bytes(fresh.at[c], forward_sems.at[0, c])

    pltpu.make_async_copy(moment1, gradient_out, store_sem.at[0]).wait()
    pltpu.make_async_copy(refreshed_out, refreshed_out, store_sem.at[3]).wait()


def relay_shards(token_grad, token_ids, block_counts, hidden, dlogits, master, moment1, moment2):
    owners = lax.axis_size("vocab")
    row_total, quarter = token_grad.shape
    blocks = row_total // BLOCK
    capacity = max(1, 2 * blocks // owners)
    slab_rows = master.shape[0]
    tokens, width = hidden.shape
    chunks = quarter // LANES
    slots = capacity * BLOCK
    f32, bf16, i32 = jnp.float32, jnp.bfloat16, jnp.int32
    hbm = pl.BlockSpec(memory_space=pl.ANY)
    dma = pltpu.SemaphoreType.DMA
    slab = (slab_rows, quarter)
    piece = (slab_rows, LANES)
    gradient, refreshed = pl.pallas_call(
        functools.partial(relay_kernel, capacity),
        out_shape=(
            jax.ShapeDtypeStruct(slab, f32),
            jax.ShapeDtypeStruct((slab_rows, width), bf16),
        ),
        in_specs=[
            pl.BlockSpec(memory_space=pltpu.SMEM),
            pl.BlockSpec(memory_space=pltpu.VMEM),
            hbm, hbm, hbm, hbm, hbm, hbm,
        ],
        out_specs=(hbm, hbm),
        scratch_shapes=[
            pltpu.SMEM((owners,), i32),
            pltpu.VMEM((blocks, BLOCK, quarter), bf16),
            pltpu.VMEM((tokens, width), bf16),
            pltpu.VMEM((slab_rows, tokens), bf16),
            pltpu.VMEM(slab, f32),
            pltpu.VMEM(slab, f32),
            pltpu.VMEM(slab, f32),
            pltpu.SMEM((8, BLOCK), i32),
            pltpu.SMEM((owners,), i32),
            pltpu.VMEM((8, BLOCK), i32),
            pltpu.VMEM((8, BLOCK), i32),
            pltpu.VMEM((3, blocks + 8, BLOCK), i32),
            pltpu.VMEM((3, blocks + 8, BLOCK), i32),
            pltpu.VMEM((chunks, 3, slots, LANES), bf16),
            pltpu.VMEM((chunks, 3, slots, LANES), bf16),
            pltpu.VMEM((chunks, blocks, BLOCK, LANES), bf16),
            pltpu.VMEM((blocks, BLOCK, LANES), bf16),
            pltpu.VMEM((4, slots, LANES), bf16),
            pltpu.VMEM((slab_rows, 4 * slots), bf16),
            pltpu.VMEM((4, slab_rows, 2 * slots), bf16),
            pltpu.VMEM(piece, f32),
            pltpu.VMEM((2, 2) + piece, f32),
            pltpu.VMEM((chunks, 2) + piece, bf16),
            pltpu.VMEM((chunks, 2) + piece, bf16),
            pltpu.VMEM((chunks, 2) + piece, bf16),
            pltpu.VMEM((chunks,) + piece, bf16),
            pltpu.VMEM((chunks, 2) + piece, bf16),
            pltpu.VMEM((chunks, 2) + piece, bf16),
            pltpu.VMEM((chunks,) + piece, bf16),
            pltpu.VMEM((chunks,) + piece, bf16),
            pltpu.VMEM((chunks,) + piece, f32),
            pltpu.VMEM((chunks,) + piece, bf16),
            pltpu.VMEM((chunks, 3) + piece, bf16),
            dma((7,)),
            dma((4,)),
            dma((2,)),
            dma((2,)),
        ]
        + [dma((2, chunks)) for _ in range(9)],
        compiler_params=pltpu.CompilerParams(
            collective_id=1, has_side_effects=True, vmem_limit_bytes=58 * 1024 * 1024
        ),
    )(
        block_counts,
        token_ids.reshape(blocks, BLOCK),
        token_grad.reshape(blocks, BLOCK, quarter),
        hidden,
        dlogits.T,
        master,
        moment1,
        moment2,
    )
    new_moment1 = beta_first * moment1 + (1.0 - beta_first) * gradient
    new_moment2 = beta_second * moment2 + (1.0 - beta_second) * gradient * gradient
    new_master = master - learn_rate * (new_moment1 / first_fix) / (
        jnp.sqrt(new_moment2 / second_fix) + adam_epsilon
    )
    return (new_master, new_moment1, new_moment2, refreshed)


def shards(*arrays):
    if lax.axis_size("vocab") == 8 and lax.axis_size("section") == 4:
        return relay_shards(*arrays)
    return direct_shards(*arrays)


def solution(mesh):
    placed = (
        P("vocab", "section"),
        P("vocab"),
        P("vocab", None),
        P("section", None),
        P("section", "vocab"),
        P("vocab", "section"),
        P("vocab", "section"),
        P("vocab", "section"),
    )
    return jax.shard_map(
        shards,
        mesh=mesh,
        in_specs=placed,
        out_specs=(
            P("vocab", "section"),
            P("vocab", "section"),
            P("vocab", "section"),
            P("vocab", None),
        ),
        check_vma=False,
    )
```

```python
import functools

import jax
import jax.numpy as jnp
from jax import lax
from jax.experimental import pallas as pl
from jax.experimental.pallas import tpu as pltpu
from jax.sharding import PartitionSpec as P

BLOCK = 128
LANES = 128
MESH = pl.DeviceIdType.MESH


beta_first = 0.9
beta_second = 0.999
learn_rate = 0.01
adam_epsilon = 1e-08
first_fix = 1.0 - 0.9**10
second_fix = 1.0 - 0.999**10


def direct_kernel(
    owners, sections, capacity,
    counts_ref, ids_ref, grad_hbm, hidden_hbm, dlogits_hbm, master_hbm, moment1_hbm, moment2_hbm,
    master_out, moment1_out, moment2_out, refreshed_out,
    starts, grad, hidden, dlogits, master, moment1, moment2,
    id_send, id_got, row_send, row_got, one_hot, part, part_got, own_part, fresh, fresh_got,
    load_sem, store_sem, id_send_sem, id_recv_sem, row_send_sem, row_recv_sem,
    part_send_sem, part_recv_sem, fresh_send_sem, fresh_recv_sem,
):
    me = lax.axis_index("vocab")
    here = lax.axis_index("section")
    quarter = master.shape[1]
    chunks = quarter // LANES
    slab_rows = master.shape[0]

    loads = [
        pltpu.make_async_copy(source, target, load_sem.at[i])
        for i, (source, target) in enumerate(
            [
                (grad_hbm, grad),
                (dlogits_hbm, dlogits),
                (hidden_hbm, hidden),
                (master_hbm, master),
                (moment1_hbm, moment1),
                (moment2_hbm, moment2),
            ]
        )
    ]
    for load in loads:
        load.start()

    barrier = pltpu.get_barrier_semaphore()

    @pl.loop(1, owners)
    def _(d):
        pl.semaphore_signal(
            barrier, inc=1, device_id={"vocab": lax.rem(me + d, owners)}, device_id_type=MESH
        )

    @pl.loop(1, sections)
    def _(e):
        pl.semaphore_signal(
            barrier, inc=1, device_id={"section": lax.rem(here + e, sections)}, device_id_type=MESH
        )

    def add_start(o, total):
        starts[o] = total
        return total + counts_ref[0, o]

    lax.fori_loop(0, owners, add_start, jnp.int32(0))

    def pick(owner, slot):
        live = slot < counts_ref[0, owner]
        return live, jnp.where(live, starts[owner] + slot, 0)

    def fill_ids(owner, target):
        target[...] = jnp.full((8, BLOCK), -1, jnp.int32)
        for slot in range(capacity):
            live, block = pick(owner, slot)
            target[slot : slot + 1, :] = jnp.where(live, ids_ref[pl.ds(block, 1), :], -1)

    pl.semaphore_wait(barrier, owners - 1 + sections - 1)

    def id_copy(d):
        return pltpu.make_async_remote_copy(
            src_ref=id_send.at[d - 1],
            dst_ref=id_got.at[d - 1],
            send_sem=id_send_sem,
            recv_sem=id_recv_sem,
            device_id={"vocab": lax.rem(me + d, owners)},
            device_id_type=MESH,
        )

    @pl.loop(1, owners)
    def _(d):
        fill_ids(lax.rem(me + d, owners), id_send.at[d - 1])
        id_copy(d).start()

    fill_ids(me, id_got.at[owners - 1])

    loads[0].wait()

    def fill_rows(owner, c, target):
        for slot in range(capacity):
            _, block = pick(owner, slot)
            target[slot * BLOCK : (slot + 1) * BLOCK, :] = grad[
                block, :, pl.ds(pl.multiple_of(c * LANES, LANES), LANES)
            ]

    @pl.loop(0, chunks)
    def _(c):
        @pl.loop(1, owners)
        def _(d):
            owner = lax.rem(me + d, owners)
            fill_rows(owner, c, row_send.at[c, d - 1])
            pltpu.make_async_remote_copy(
                src_ref=row_send.at[c, d - 1],
                dst_ref=row_got.at[c, d - 1],
                send_sem=row_send_sem.at[c],
                recv_sem=row_recv_sem.at[c],
                device_id={"vocab": owner},
                device_id_type=MESH,
            ).start()

        fill_rows(me, c, row_got.at[c, owners - 1])

    loads[1].wait()
    loads[2].wait()

    def head_part(section, c):
        at = pl.multiple_of(section * quarter + c * LANES, LANES)
        return jnp.dot(
            dlogits[...], hidden[:, pl.ds(at, LANES)], preferred_element_type=jnp.float32
        )

    @pl.loop(0, chunks)
    def _(c):
        @pl.loop(1, sections)
        def _(e):
            section = lax.rem(here + e, sections)
            part[c, e - 1] = head_part(section, c).astype(jnp.bfloat16)
            pltpu.make_async_remote_copy(
                src_ref=part.at[c, e - 1],
                dst_ref=part_got.at[c, e - 1],
                send_sem=part_send_sem.at[c],
                recv_sem=part_recv_sem.at[c],
                device_id={"section": section},
                device_id_type=MESH,
            ).start()

        own_part[c] = head_part(here, c)

    arrived = id_got.at[pl.ds(0, owners - 1)]
    pltpu.make_async_copy(arrived, arrived, id_recv_sem).wait()

    @pl.loop(0, owners)
    def _(s):
        for slot in range(capacity):
            ids = id_got[s, slot : slot + 1, :]
            rows = lax.broadcasted_iota(jnp.int32, (slab_rows, BLOCK), 0)
            at = pl.multiple_of((s * capacity + slot) * BLOCK, BLOCK)
            one_hot[:, pl.ds(at, BLOCK)] = jnp.where(rows == ids, 1.0, 0.0).astype(jnp.bfloat16)

    for load in loads[3:]:
        load.wait()

    @pl.loop(0, chunks)
    def _(c):
        cols = pl.ds(pl.multiple_of(c * LANES, LANES), LANES)
        rows_in = row_got.at[c, pl.ds(0, owners - 1)]
        pltpu.make_async_copy(rows_in, rows_in, row_recv_sem.at[c]).wait()
        parts_in = part_got.at[c]
        pltpu.make_async_copy(parts_in, parts_in, part_recv_sem.at[c]).wait()
        gradient = jnp.dot(
            one_hot[...],
            row_got[c].reshape(owners * capacity * BLOCK, LANES),
            preferred_element_type=jnp.float32,
        )
        head = own_part[c]
        for e in range(sections - 1):
            head = head + part_got[c, e].astype(jnp.float32)
        gradient = gradient + head
        new_moment1 = beta_first * moment1[:, cols] + (1.0 - beta_first) * gradient
        new_moment2 = beta_second * moment2[:, cols] + (1.0 - beta_second) * gradient * gradient
        new_master = master[:, cols] - learn_rate * (new_moment1 / first_fix) / (
            jnp.sqrt(new_moment2 / second_fix) + adam_epsilon
        )
        fresh[c] = new_master.astype(jnp.bfloat16)

        @pl.loop(1, sections)
        def _(e):
            pltpu.make_async_remote_copy(
                src_ref=fresh.at[c],
                dst_ref=fresh_got.at[c, e - 1],
                send_sem=fresh_send_sem.at[c],
                recv_sem=fresh_recv_sem.at[c],
                device_id={"section": lax.rem(here + e, sections)},
                device_id_type=MESH,
            ).start()

        moment1[:, cols] = new_moment1
        moment2[:, cols] = new_moment2
        master[:, cols] = new_master
        pltpu.make_async_copy(master.at[:, cols], master_out.at[:, cols], store_sem.at[0]).start()
        pltpu.make_async_copy(moment1.at[:, cols], moment1_out.at[:, cols], store_sem.at[1]).start()
        pltpu.make_async_copy(moment2.at[:, cols], moment2_out.at[:, cols], store_sem.at[2]).start()
        at = pl.multiple_of(here * quarter + c * LANES, LANES)
        pltpu.make_async_copy(
            fresh.at[c], refreshed_out.at[:, pl.ds(at, LANES)], store_sem.at[3]
        ).start()

    @pl.loop(0, chunks)
    def _(c):
        fresh_in = fresh_got.at[c]
        pltpu.make_async_copy(fresh_in, fresh_in, fresh_recv_sem.at[c]).wait()

        @pl.loop(1, sections)
        def _(e):
            source = lax.rem(here + sections - e, sections)
            at = pl.multiple_of(source * quarter + c * LANES, LANES)
            pltpu.make_async_copy(
                fresh_got.at[c, e - 1], refreshed_out.at[:, pl.ds(at, LANES)], store_sem.at[3]
            ).start()

    pltpu.make_async_copy(id_send, id_send, id_send_sem).wait()

    @pl.loop(0, chunks)
    def _(c):
        pltpu.make_async_copy(row_send.at[c], row_send.at[c], row_send_sem.at[c]).wait()
        pltpu.make_async_copy(part.at[c], part.at[c], part_send_sem.at[c]).wait()
        pltpu.make_async_copy(fresh_got.at[c], fresh_got.at[c], fresh_send_sem.at[c]).wait()

    pltpu.make_async_copy(master, master_out, store_sem.at[0]).wait()
    pltpu.make_async_copy(moment1, moment1_out, store_sem.at[1]).wait()
    pltpu.make_async_copy(moment2, moment2_out, store_sem.at[2]).wait()
    pltpu.make_async_copy(refreshed_out, refreshed_out, store_sem.at[3]).wait()


def direct_shards(token_grad, token_ids, block_counts, hidden, dlogits, master, moment1, moment2):
    owners = lax.axis_size("vocab")
    sections = lax.axis_size("section")
    row_total, quarter = token_grad.shape
    block_total = row_total // BLOCK
    capacity = max(1, 2 * block_total // owners)
    slab_rows = master.shape[0]
    tokens, width = hidden.shape
    chunks = quarter // LANES
    slots = capacity * BLOCK
    f32, bf16 = jnp.float32, jnp.bfloat16
    hbm = pl.BlockSpec(memory_space=pl.ANY)
    dma = pltpu.SemaphoreType.DMA
    slab = (slab_rows, quarter)
    return pl.pallas_call(
        functools.partial(direct_kernel, owners, sections, capacity),
        out_shape=(
            jax.ShapeDtypeStruct(slab, f32),
            jax.ShapeDtypeStruct(slab, f32),
            jax.ShapeDtypeStruct(slab, f32),
            jax.ShapeDtypeStruct((slab_rows, width), bf16),
        ),
        in_specs=[
            pl.BlockSpec(memory_space=pltpu.SMEM),
            pl.BlockSpec(memory_space=pltpu.VMEM),
            hbm, hbm, hbm, hbm, hbm, hbm,
        ],
        out_specs=(hbm, hbm, hbm, hbm),
        scratch_shapes=[
            pltpu.SMEM((owners,), jnp.int32),
            pltpu.VMEM((block_total, BLOCK, quarter), bf16),
            pltpu.VMEM((tokens, width), bf16),
            pltpu.VMEM((slab_rows, tokens), bf16),
            pltpu.VMEM(slab, f32),
            pltpu.VMEM(slab, f32),
            pltpu.VMEM(slab, f32),
            pltpu.VMEM((owners - 1, 8, BLOCK), jnp.int32),
            pltpu.VMEM((owners, 8, BLOCK), jnp.int32),
            pltpu.VMEM((chunks, owners - 1, slots, LANES), bf16),
            pltpu.VMEM((chunks, owners, slots, LANES), bf16),
            pltpu.VMEM((slab_rows, owners * slots), bf16),
            pltpu.VMEM((chunks, sections - 1, slab_rows, LANES), bf16),
            pltpu.VMEM((chunks, sections - 1, slab_rows, LANES), bf16),
            pltpu.VMEM((chunks, slab_rows, LANES), f32),
            pltpu.VMEM((chunks, slab_rows, LANES), bf16),
            pltpu.VMEM((chunks, sections - 1, slab_rows, LANES), bf16),
            dma((6,)),
            dma((4,)),
            dma,
            dma,
            dma((chunks,)),
            dma((chunks,)),
            dma((chunks,)),
            dma((chunks,)),
            dma((chunks,)),
            dma((chunks,)),
        ],
        compiler_params=pltpu.CompilerParams(
            collective_id=0, has_side_effects=True, vmem_limit_bytes=58 * 1024 * 1024
        ),
    )(
        block_counts,
        token_ids.reshape(block_total, BLOCK),
        token_grad.reshape(block_total, BLOCK, quarter),
        hidden,
        dlogits.T,
        master,
        moment1,
        moment2,
    )


def relay_kernel(
    capacity,
    counts_ref, ids_ref, grad_hbm, hidden_hbm, dlogits_hbm, master_hbm, moment1_hbm, moment2_hbm,
    gradient_out, refreshed_out,
    starts, grad, hidden, dlogits, master, moment1, moment2,
    mate_counts, mate_starts, count_send, count_got, id_send, id_got, slot_send, slot_got, raw_got,
    raw_now, near_raw, near_hot, far_hot, total, far_keep, relay_send, relay_got, far_send, far_got,
    pair_send, pair_got, cross_send, cross_got, own_part, fresh, fresh_got,
    load_sem, store_sem, count_sems, id_sems, slot_sems, raw_sems, relay_sems, far_sems,
    pair_sems, cross_sems, side_sems, over_sems, forward_sems,
):
    owners = counts_ref.shape[1]
    me = lax.axis_index("vocab")
    here = lax.axis_index("section")
    z, y = me // 2, lax.rem(me, 2)
    mate_z = z + 1 - 2 * lax.rem(z, 2)
    mate = mate_z * 2 + y
    level = z * 2 + 1 - y
    corner = mate_z * 2 + 1 - y
    near = (mate, level, corner)
    inner = jnp.logical_or(z == 1, z == 2)
    outer = jnp.logical_not(inner)
    far_inner_z = 3 - z
    far_outer_z = lax.rem(z + 2, 4)
    far = (
        far_inner_z * 2 + 1 - y,
        far_outer_z * 2 + 1 - y,
        far_inner_z * 2 + y,
        far_outer_z * 2 + y,
    )
    sections = 4
    sibling = here + 1 - 2 * lax.rem(here, 2)
    across = lax.rem(here + 2, sections)
    other = lax.rem(sibling + 2, sections)
    slab_rows, quarter = master.shape
    blocks = grad.shape[0]
    chunks = quarter // LANES
    slots = capacity * BLOCK

    loads = [
        pltpu.make_async_copy(source, target, load_sem.at[i])
        for i, (source, target) in enumerate(
            [
                (grad_hbm, grad),
                (dlogits_hbm, dlogits),
                (hidden_hbm, hidden),
                (master_hbm, master),
                (moment1_hbm, moment1),
                (moment2_hbm, moment2),
            ]
        )
    ]
    for load in loads:
        load.start()

    barrier = pltpu.get_barrier_semaphore()

    @pl.loop(1, owners)
    def _(d):
        pl.semaphore_signal(
            barrier, inc=1, device_id={"vocab": lax.rem(me + d, owners)}, device_id_type=MESH
        )

    @pl.loop(1, sections)
    def _(e):
        pl.semaphore_signal(
            barrier, inc=1, device_id={"section": lax.rem(here + e, sections)}, device_id_type=MESH
        )

    def send(source, target, sems, where, c=None):
        return pltpu.make_async_remote_copy(
            src_ref=source,
            dst_ref=target,
            send_sem=sems.at[0] if c is None else sems.at[0, c],
            recv_sem=sems.at[1] if c is None else sems.at[1, c],
            device_id=where,
            device_id_type=MESH,
        ).start()

    def await_bytes(ref, sem):
        pltpu.make_async_copy(ref, ref, sem).wait()

    def sum_starts(target, counts):
        def add_start(o, so_far):
            target[o] = so_far
            return so_far + counts[0, o]

        lax.fori_loop(0, owners, add_start, jnp.int32(0))

    def pick_from(counts, first, owner, slot):
        live = slot < counts[0, owner]
        return live, jnp.where(live, first[owner] + slot, 0)

    def pick(owner, slot):
        return pick_from(counts_ref, starts, owner, slot)

    def mate_pick(owner, slot):
        return pick_from(mate_counts, mate_starts, owner, slot)

    sum_starts(starts, counts_ref)

    def own_ids(owner, slot):
        live, block = pick(owner, slot)
        return jnp.where(live, ids_ref[pl.ds(block, 1), :], -1)

    lanes = lax.broadcasted_iota(jnp.int32, (8, BLOCK), 1)
    count_row = jnp.zeros((8, BLOCK), jnp.int32)
    for o in range(owners):
        count_row = jnp.where(lanes == o, counts_ref[0, o], count_row)
    count_send[...] = count_row

    for i, owner in enumerate(near):
        id_send[i, 0:blocks, :] = ids_ref[...]
        id_send[i, blocks:, :] = jnp.full((8, BLOCK), -1, jnp.int32)
        for slot in range(capacity):
            row = blocks + slot
            id_send[i, row : row + 1, :] = own_ids(owner, slot)

    pl.semaphore_wait(barrier, owners - 1 + sections - 1)

    for i, owner in enumerate(near):
        send(id_send.at[i], id_got.at[i], id_sems, {"vocab": owner})

    send(count_send, count_got, count_sems, {"vocab": mate})

    loads[0].wait()

    def columns(c):
        return pl.ds(pl.multiple_of(c * LANES, LANES), LANES)

    def send_slot(i, c):
        for slot in range(capacity):
            _, block = pick(near[i], slot)
            slot_send[c, i, slot * BLOCK : (slot + 1) * BLOCK, :] = grad[block, :, columns(c)]
        send(slot_send.at[c, i], slot_got.at[c, i], slot_sems, {"vocab": near[i]}, c)

    @pl.loop(0, chunks)
    def _(c):
        @pl.when(outer)
        def _():
            send(grad.at[:, :, columns(c)], raw_got.at[c], raw_sems, {"vocab": mate}, c)

        @pl.when(inner)
        def _():
            send_slot(0, c)

        send_slot(1, c)
        send_slot(2, c)

    loads[1].wait()
    loads[2].wait()

    def head_part(section, c):
        at = pl.multiple_of(section * quarter + c * LANES, LANES)
        return jnp.dot(
            dlogits[...], hidden[:, pl.ds(at, LANES)], preferred_element_type=jnp.float32
        )

    @pl.loop(0, chunks)
    def _(c):
        pair_send[c, 0] = head_part(sibling, c).astype(jnp.bfloat16)
        pair_send[c, 1] = head_part(other, c).astype(jnp.bfloat16)
        send(pair_send.at[c], pair_got.at[c], pair_sems, {"section": sibling}, c)

    def one_hot(ids):
        rows = lax.broadcasted_iota(jnp.int32, (slab_rows, BLOCK), 0)
        return jnp.where(rows == ids, 1.0, 0.0).astype(jnp.bfloat16)

    await_bytes(id_got, id_sems.at[1])
    await_bytes(count_got, count_sems.at[1])

    @pl.when(inner)
    def _():
        to_scalars = pltpu.make_async_copy(count_got, mate_counts, load_sem.at[6])
        to_scalars.start()
        to_scalars.wait()
        sum_starts(mate_starts, mate_counts)
        for f in range(4):
            for slot in range(capacity):
                at = slot * BLOCK
                far_hot[f, :, at : at + BLOCK] = one_hot(own_ids(far[f], slot))
                live, block = mate_pick(far[f], slot)
                ids = jnp.where(live, id_got[0, pl.ds(block, 1), :], -1)
                at = slots + slot * BLOCK
                far_hot[f, :, at : at + BLOCK] = one_hot(ids)

    @pl.loop(0, chunks)
    def _(c):
        own_part[c] = head_part(here, c)
        mine = head_part(across, c)
        await_bytes(pair_got.at[c], pair_sems.at[1, c])
        cross_send[c] = (mine + pair_got[c, 1].astype(jnp.float32)).astype(jnp.bfloat16)
        send(cross_send.at[c], cross_got.at[c], cross_sems, {"section": across}, c)

    for slot in range(capacity):
        at = slot * BLOCK
        near_hot[:, at : at + BLOCK] = one_hot(own_ids(me, slot))
        for i in range(3):
            at = ((i + 1) * capacity + slot) * BLOCK
            row = blocks + slot
            near_hot[:, at : at + BLOCK] = one_hot(id_got[i, row : row + 1, :])

    for load in loads[3:]:
        load.wait()

    def dot(a, b):
        return jnp.dot(a, b, preferred_element_type=jnp.float32)

    def own_rows(owner, c):
        return [grad[pick(owner, slot)[1], :, columns(c)] for slot in range(capacity)]

    def raw_rows(owner):
        return [raw_now[mate_pick(owner, slot)[1]] for slot in range(capacity)]

    def far_sum(f, c):
        rows = jnp.concatenate(own_rows(far[f], c) + raw_rows(far[f]), axis=0)
        return dot(far_hot[f], rows)

    def gather_far(c):
        await_bytes(raw_got.at[c], raw_sems.at[1, c])
        raw_now[...] = raw_got[c]
        near_raw[lax.rem(c, 4)] = jnp.concatenate(raw_rows(me), axis=0)
        for f in range(2):
            relay_send[c, f] = far_sum(f, c).astype(jnp.bfloat16)
        send(relay_send.at[c], relay_got.at[c], relay_sems, {"vocab": level}, c)
        for f in range(2):
            far_keep[lax.rem(c, 2), f] = far_sum(2 + f, c)

    def send_far(c):
        await_bytes(relay_got.at[c], relay_sems.at[1, c])
        for f in range(2):
            far_send[c, f] = (
                far_keep[lax.rem(c, 2), f] + relay_got[c, f].astype(jnp.float32)
            ).astype(jnp.bfloat16)
            send(far_send.at[c, f], far_got.at[c], far_sems, {"vocab": far[2 + f]}, c)

    def update(c):
        cols = columns(c)
        await_bytes(far_got.at[c], far_sems.at[1, c])
        await_bytes(cross_got.at[c], cross_sems.at[1, c])

        @pl.when(inner)
        def _():
            await_bytes(slot_got.at[c, pl.ds(1, 2)], slot_sems.at[1, c])
            rest = slot_got[c, 1:3].reshape(2 * slots, LANES)
            rows = jnp.concatenate(own_rows(me, c) + [near_raw[lax.rem(c, 4)], rest], axis=0)
            total[...] = dot(near_hot[...], rows)

        @pl.when(outer)
        def _():
            await_bytes(slot_got.at[c], slot_sems.at[1, c])
            rest = slot_got[c].reshape(3 * slots, LANES)
            total[...] = dot(near_hot[...], jnp.concatenate(own_rows(me, c) + [rest], axis=0))

        gradient = (
            total[...]
            + far_got[c].astype(jnp.float32)
            + own_part[c]
            + pair_got[c, 0].astype(jnp.float32)
            + cross_got[c].astype(jnp.float32)
        )
        new_moment1 = beta_first * moment1[:, cols] + (1.0 - beta_first) * gradient
        new_moment2 = beta_second * moment2[:, cols] + (1.0 - beta_second) * gradient * gradient
        new_master = master[:, cols] - learn_rate * (new_moment1 / first_fix) / (
            jnp.sqrt(new_moment2 / second_fix) + adam_epsilon
        )
        fresh[c] = new_master.astype(jnp.bfloat16)
        send(fresh.at[c], fresh_got.at[c, 1], over_sems, {"section": across}, c)
        send(fresh.at[c], fresh_got.at[c, 0], side_sems, {"section": sibling}, c)
        moment1[:, cols] = gradient
        pltpu.make_async_copy(
            moment1.at[:, cols], gradient_out.at[:, cols], store_sem.at[0]
        ).start()
        store_fresh(fresh.at[c], here, c)

    def store_fresh(source, section, c):
        at = pl.multiple_of(section * quarter + c * LANES, LANES)
        pltpu.make_async_copy(
            source, refreshed_out.at[:, pl.ds(at, LANES)], store_sem.at[3]
        ).start()

    def forward(c):
        await_bytes(fresh_got.at[c, 1], over_sems.at[1, c])
        send(fresh_got.at[c, 1], fresh_got.at[c, 2], forward_sems, {"section": sibling}, c)
        store_fresh(fresh_got.at[c, 1], across, c)
        await_bytes(fresh_got.at[c, 0], side_sems.at[1, c])
        store_fresh(fresh_got.at[c, 0], sibling, c)

    def finish(c):
        await_bytes(fresh_got.at[c, 2], forward_sems.at[1, c])
        store_fresh(fresh_got.at[c, 2], other, c)

    @pl.loop(0, chunks + 6)
    def _(t):
        @pl.when(jnp.logical_and(inner, t < chunks))
        def _():
            gather_far(t)

        @pl.when(jnp.logical_and(inner, jnp.logical_and(t >= 1, t < chunks + 1)))
        def _():
            send_far(t - 1)

        @pl.when(jnp.logical_and(t >= 3, t < chunks + 3))
        def _():
            update(t - 3)

        @pl.when(jnp.logical_and(t >= 5, t < chunks + 5))
        def _():
            forward(t - 5)

        @pl.when(t >= 6)
        def _():
            finish(t - 6)

    await_bytes(id_send, id_sems.at[0])
    await_bytes(count_send, count_sems.at[0])

    @pl.loop(0, chunks)
    def _(c):
        @pl.when(outer)
        def _():
            await_bytes(raw_got.at[c], raw_sems.at[0, c])
            await_bytes(slot_send.at[c, pl.ds(1, 2)], slot_sems.at[0, c])

        @pl.when(inner)
        def _():
            await_bytes(slot_send.at[c], slot_sems.at[0, c])
            await_bytes(relay_send.at[c], relay_sems.at[0, c])
            await_bytes(far_send.at[c], far_sems.at[0, c])

        await_bytes(pair_send.at[c], pair_sems.at[0, c])
        await_bytes(cross_send.at[c], cross_sems.at[0, c])
        await_bytes(fresh.at[c], side_sems.at[0, c])
        await_bytes(fresh.at[c], over_sems.at[0, c])
        await_bytes(fresh.at[c], forward_sems.at[0, c])

    pltpu.make_async_copy(moment1, gradient_out, store_sem.at[0]).wait()
    pltpu.make_async_copy(refreshed_out, refreshed_out, store_sem.at[3]).wait()


def relay_shards(token_grad, token_ids, block_counts, hidden, dlogits, master, moment1, moment2):
    owners = lax.axis_size("vocab")
    row_total, quarter = token_grad.shape
    blocks = row_total // BLOCK
    capacity = max(1, 2 * blocks // owners)
    slab_rows = master.shape[0]
    tokens, width = hidden.shape
    chunks = quarter // LANES
    slots = capacity * BLOCK
    f32, bf16, i32 = jnp.float32, jnp.bfloat16, jnp.int32
    hbm = pl.BlockSpec(memory_space=pl.ANY)
    dma = pltpu.SemaphoreType.DMA
    slab = (slab_rows, quarter)
    piece = (slab_rows, LANES)
    gradient, refreshed = pl.pallas_call(
        functools.partial(relay_kernel, capacity),
        out_shape=(
            jax.ShapeDtypeStruct(slab, f32),
            jax.ShapeDtypeStruct((slab_rows, width), bf16),
        ),
        in_specs=[
            pl.BlockSpec(memory_space=pltpu.SMEM),
            pl.BlockSpec(memory_space=pltpu.VMEM),
            hbm, hbm, hbm, hbm, hbm, hbm,
        ],
        out_specs=(hbm, hbm),
        scratch_shapes=[
            pltpu.SMEM((owners,), i32),
            pltpu.VMEM((blocks, BLOCK, quarter), bf16),
            pltpu.VMEM((tokens, width), bf16),
            pltpu.VMEM((slab_rows, tokens), bf16),
            pltpu.VMEM(slab, f32),
            pltpu.VMEM(slab, f32),
            pltpu.VMEM(slab, f32),
            pltpu.SMEM((8, BLOCK), i32),
            pltpu.SMEM((owners,), i32),
            pltpu.VMEM((8, BLOCK), i32),
            pltpu.VMEM((8, BLOCK), i32),
            pltpu.VMEM((3, blocks + 8, BLOCK), i32),
            pltpu.VMEM((3, blocks + 8, BLOCK), i32),
            pltpu.VMEM((chunks, 3, slots, LANES), bf16),
            pltpu.VMEM((chunks, 3, slots, LANES), bf16),
            pltpu.VMEM((chunks, blocks, BLOCK, LANES), bf16),
            pltpu.VMEM((blocks, BLOCK, LANES), bf16),
            pltpu.VMEM((4, slots, LANES), bf16),
            pltpu.VMEM((slab_rows, 4 * slots), bf16),
            pltpu.VMEM((4, slab_rows, 2 * slots), bf16),
            pltpu.VMEM(piece, f32),
            pltpu.VMEM((2, 2) + piece, f32),
            pltpu.VMEM((chunks, 2) + piece, bf16),
            pltpu.VMEM((chunks, 2) + piece, bf16),
            pltpu.VMEM((chunks, 2) + piece, bf16),
            pltpu.VMEM((chunks,) + piece, bf16),
            pltpu.VMEM((chunks, 2) + piece, bf16),
            pltpu.VMEM((chunks, 2) + piece, bf16),
            pltpu.VMEM((chunks,) + piece, bf16),
            pltpu.VMEM((chunks,) + piece, bf16),
            pltpu.VMEM((chunks,) + piece, f32),
            pltpu.VMEM((chunks,) + piece, bf16),
            pltpu.VMEM((chunks, 3) + piece, bf16),
            dma((7,)),
            dma((4,)),
            dma((2,)),
            dma((2,)),
        ]
        + [dma((2, chunks)) for _ in range(9)],
        compiler_params=pltpu.CompilerParams(
            collective_id=1, has_side_effects=True, vmem_limit_bytes=58 * 1024 * 1024
        ),
    )(
        block_counts,
        token_ids.reshape(blocks, BLOCK),
        token_grad.reshape(blocks, BLOCK, quarter),
        hidden,
        dlogits.T,
        master,
        moment1,
        moment2,
    )
    new_moment1 = beta_first * moment1 + (1.0 - beta_first) * gradient
    new_moment2 = beta_second * moment2 + (1.0 - beta_second) * gradient * gradient
    new_master = master - learn_rate * (new_moment1 / first_fix) / (
        jnp.sqrt(new_moment2 / second_fix) + adam_epsilon
    )
    return (new_master, new_moment1, new_moment2, refreshed)


def shards(*arrays):
    if lax.axis_size("vocab") == 8 and lax.axis_size("section") == 4:
        return relay_shards(*arrays)
    return direct_shards(*arrays)


def solution(mesh):
    placed = (
        P("vocab", "section"),
        P("vocab"),
        P("vocab", None),
        P("section", None),
        P("section", "vocab"),
        P("vocab", "section"),
        P("vocab", "section"),
        P("vocab", "section"),
    )
    return jax.shard_map(
        shards,
        mesh=mesh,
        in_specs=placed,
        out_specs=(
            P("vocab", "section"),
            P("vocab", "section"),
            P("vocab", "section"),
            P("vocab", None),
        ),
        check_vma=False,
    )
```
